128 devices in a mesh: gx: 8 (over z, x_lo), gy: 4 (over x_hi, core), gz: 4 (over y).
Axes of the slice: x: 4 (x_hi: 2, x_lo: 2; x = x_hi * 2 + x_lo), y: 4, z: 4, core: 2. Of those that a mesh axis runs over, the one named last changes fastest.
Arguments:
- volume: bfloat16 [64, 128, 512], P('gx', 'gy', 'gz'), may hold values from -60 to 60
- conv_one: bfloat16 [3, 3, 3, 1, 16], replicated, may hold values from -1.25 to 1.25
- gain_one: float32 [16], replicated, may hold values from 0.1 to 1.9
- shift_one: float32 [16], replicated, may hold values from -3 to 3
- second_level_kernel: bfloat16 [3, 3, 3, 16, 32], replicated, may hold values from -0.3125 to 0.3125
- second_level_gain: float32 [32], replicated, may hold values from 0.1 to 1.9
- second_level_bias: float32 [32], replicated, may hold values from -3 to 3
- third_level_kernel: bfloat16 [3, 3, 3, 32, 64], replicated, may hold values from -0.21875 to 0.21875
- third_level_gain: float32 [64], replicated, may hold values from 0.1 to 1.9
- third_level_bias: float32 [64], replicated, may hold values from -3 to 3
- bottleneck_kernel: bfloat16 [3, 3, 3, 64, 128], replicated, may hold values from -0.15625 to 0.15625
- bottleneck_norm_gain: float32 [128], replicated, may hold values from 0.1 to 1.9
- bottleneck_norm_bias: float32 [128], replicated, may hold values from -3 to 3
Outputs:
- first_level_features: bfloat16 [64, 128, 8192], P('gx', 'gy', 'gz')
- second_level_features: bfloat16 [32, 64, 8192], P('gx', 'gy', 'gz')
- third_level_features: bfloat16 [16, 32, 8192], P('gx', 'gy', 'gz')
- bottleneck: bfloat16 [8, 16, 8192], replicated
The draws below stay inside these ranges and needn't reach their ends.
All inputs are finite; a program needn't handle non-finite values.
Results may differ from the reference program's by a relative error of at most 0.012.
The reference program's roundings to bfloat16 on the way count: a program that leaves them out, or rounds other values in their place, can miss the bound.
Values may be sent and summed in bfloat16 or wider, within the bound.
No kernel may reach another device: no remote copies, remote signals or barrier semaphores. Data moves between devices by JAX's collectives and lax.ppermute only.
A program may use at most 128 MiB of HBM per device.

```python
import jax
import jax.numpy as jnp
from jax import lax

FIRST_CHANNELS = 16
SECOND_CHANNELS = 32
THIRD_CHANNELS = 64
C4 = 128
NX = 64
NY = 128
NZ = 512


def draw_volume(key, part):
    key = jax.random.fold_in(key, 11)
    first = jax.random.fold_in(key, 0)
    position = jnp.arange(NX, dtype=jnp.float32) / float(max(NX - 1, 1))
    ramp = jnp.exp(jnp.log(3.0) * position)[:, None, None]
    base = jnp.clip(jax.random.normal(first, (NX, NY, NZ), jnp.float32), -6.0, 6.0)
    values = base * ramp
    return values.astype(jnp.bfloat16)


def normal_values(stream_key, shape, spread, most, kind=jnp.bfloat16):
    entries = jax.random.normal(stream_key, shape, jnp.float32) * spread
    return jnp.minimum(jnp.maximum(entries, -most), most).astype(kind)


def setup_inputs(seed: int = 0) -> dict:
    arg_keys = jax.random.split(jax.random.key(seed), 14)
    return {
        "volume": draw_volume(jax.random.fold_in(arg_keys[13], 71), 0),
        "conv_one": normal_values(arg_keys[1], (3, 3, 3, 1, FIRST_CHANNELS), 27 ** -0.5, 1.25),
        "gain_one": jnp.clip(1.0 + 0.18 * jax.random.normal(arg_keys[2], (FIRST_CHANNELS,), jnp.float32), 0.1, 1.9),
        "shift_one": normal_values(arg_keys[3], (FIRST_CHANNELS,), 0.5, 3.0, jnp.float32),
        "second_level_kernel": normal_values(arg_keys[4], (3, 3, 3, FIRST_CHANNELS, SECOND_CHANNELS), (27 * FIRST_CHANNELS) ** -0.5, 0.3125),
        "second_level_gain": jnp.clip(1.0 + 0.18 * jax.random.normal(arg_keys[5], (SECOND_CHANNELS,), jnp.float32), 0.1, 1.9),
        "second_level_bias": normal_values(arg_keys[6], (SECOND_CHANNELS,), 0.5, 3.0, jnp.float32),
        "third_level_kernel": normal_values(arg_keys[7], (3, 3, 3, SECOND_CHANNELS, THIRD_CHANNELS), (27 * SECOND_CHANNELS) ** -0.5, 0.21875),
        "third_level_gain": jnp.clip(1.0 + 0.18 * jax.random.normal(arg_keys[8], (THIRD_CHANNELS,), jnp.float32), 0.1, 1.9),
        "third_level_bias": normal_values(arg_keys[9], (THIRD_CHANNELS,), 0.5, 3.0, jnp.float32),
        "bottleneck_kernel": normal_values(arg_keys[10], (3, 3, 3, THIRD_CHANNELS, C4), (27 * THIRD_CHANNELS) ** -0.5, 0.15625),
        "bottleneck_norm_gain": jnp.clip(1.0 + 0.18 * jax.random.normal(arg_keys[11], (C4,), jnp.float32), 0.1, 1.9),
        "bottleneck_norm_bias": normal_values(arg_keys[12], (C4,), 0.5, 3.0, jnp.float32),
    }


EPSILON = 1e-05

def conv_same(input_volume, weight):
    chans_in = weight.shape[3]
    chans_out = weight.shape[4]
    sx, sy, merged = input_volume.shape
    shaped = input_volume.reshape(1, sx, sy, merged // chans_in, chans_in).astype(jnp.float32)
    result = lax.conv_general_dilated(shaped, weight.astype(jnp.float32), (1, 1, 1), 'SAME', dimension_numbers=('NDHWC', 'DHWIO', 'NDHWC'), precision=lax.Precision.HIGHEST)
    return result.reshape(sx, sy, merged // chans_in * chans_out)

def settle(response, totals, cells_total, scale_gain, shift_vec):
    channel_list = scale_gain.shape[0]
    mean_vec = totals[0] / cells_total
    variance = totals[1] / cells_total - mean_vec * mean_vec
    factor = scale_gain * lax.rsqrt(variance + EPSILON)
    flat = response.reshape(-1, channel_list)
    normed = (flat - mean_vec[None, :]) * factor[None, :] + shift_vec[None, :]
    return jax.nn.relu(normed).astype(jnp.bfloat16).reshape(response.shape)

def halve_resolution(input_volume, channel_list):
    sx, sy, merged = input_volume.shape
    sz = merged // channel_list
    pooled = lax.optimization_barrier(jnp.max(input_volume.reshape(sx // 2, 2, sy // 2, 2, sz // 2, 2, channel_list), axis=(1, 3, 5)))
    return pooled.reshape(sx // 2, sy // 2, sz // 2 * channel_list)

def apply_encoder_level(input_volume, weight, scale_gain, shift_vec):
    channel_list = weight.shape[4]
    response = conv_same(input_volume, weight)
    flat = response.reshape(-1, channel_list)
    totals = (lax.optimization_barrier(jnp.sum(flat, axis=0)), lax.optimization_barrier(jnp.sum(flat * flat, axis=0)))
    cells_total = float(flat.shape[0])
    return settle(response, totals, cells_total, scale_gain, shift_vec)

def reference(volume, conv_one, gain_one, shift_one, second_level_kernel, second_level_gain, second_level_bias, third_level_kernel, third_level_gain, third_level_bias, bottleneck_kernel, bottleneck_norm_gain, bottleneck_norm_bias):
    first_level_features = apply_encoder_level(volume, conv_one, gain_one, shift_one)
    second_level_features = apply_encoder_level(halve_resolution(first_level_features, FIRST_CHANNELS), second_level_kernel, second_level_gain, second_level_bias)
    third_level_features = apply_encoder_level(halve_resolution(second_level_features, SECOND_CHANNELS), third_level_kernel, third_level_gain, third_level_bias)
    bottleneck = apply_encoder_level(halve_resolution(third_level_features, THIRD_CHANNELS), bottleneck_kernel, bottleneck_norm_gain, bottleneck_norm_bias)
    return (first_level_features, second_level_features, third_level_features, bottleneck)
```

```python
import jax
import jax.numpy as jnp
from jax import lax
from jax.experimental import pallas as pl
from jax.experimental.pallas import tpu as pltpu
from jax.sharding import PartitionSpec as P

EPSILON = 1e-05
F32 = jnp.float32
BF16 = jnp.bfloat16
AXES = ("gx", "gy", "gz")
DEVICES = 128
VOXELS_1 = 64.0 * 128.0 * 512.0
PARAMS = pltpu.CompilerParams(vmem_limit_bytes=56 * 1024 * 1024)


def full(shape, dtype):
    return jax.ShapeDtypeStruct(shape, dtype)


def iota(shape, dim):
    return lax.broadcasted_iota(jnp.int32, shape, dim)


def band_kernel(k1_ref, k2_ref, k3_ref, k4_ref, w1_ref, w2_ref, w3_ref, w4_ref, t2_ref, t3_ref):
    spread = (iota((16, 768), 1) % 16 == iota((16, 768), 0)).astype(BF16)
    taps = jnp.dot(k1_ref[...], spread, preferred_element_type=F32)
    lag = iota((64, 768), 0) - iota((64, 768), 1) // 16
    for dx in range(3):
        for dy in range(3):
            block = jnp.zeros((64, 768), F32)
            for dz in range(3):
                t = (dx * 3 + dy) * 3 + dz
                block = jnp.where(lag == dz, taps[t : t + 1, :], block)
            w1_ref[dx * 256 + dy * 64 : dx * 256 + dy * 64 + 64, :] = block.astype(BF16)
        w1_ref[dx * 256 + 192 : dx * 256 + 256, :] = jnp.zeros((64, 768), BF16)

    def banded(k_ref, w_ref, t_ref, cin, cout, first):
        outs = 256 // cout
        if outs > 1:
            tile = (iota((cout, 256), 1) % cout == iota((cout, 256), 0)).astype(BF16)
            t_ref[...] = jnp.dot(k_ref[...], tile, preferred_element_type=F32)
        zo = iota((cin, 256), 1) // cout

        def plane(p, carry):
            for zi in range(-first, 256 // cin - first):
                block = jnp.zeros((cin, 256), F32)
                if 0 <= zi < outs + 2:
                    for dz in range(3):
                        start = pl.multiple_of((p * 3 + dz) * cin, cin)
                        block = jnp.where(zo == zi - dz, t_ref[pl.ds(start, cin), :], block)
                start = pl.multiple_of(p * 256 + (zi + first) * cin, cin)
                w_ref[pl.ds(start, cin), :] = block.astype(BF16)
            return carry

        lax.fori_loop(0, 9, plane, 0)

    banded(k2_ref, w2_ref, t2_ref, 16, 32, 1)
    banded(k3_ref, w3_ref, t3_ref.at[0:864], 32, 64, 0)
    banded(k4_ref, w4_ref, t3_ref, 64, 128, 0)


def bands(k1, k2, k3, k4):
    return pl.pallas_call(
        band_kernel,
        out_shape=(
            full((768, 768), BF16),
            full((2304, 256), BF16),
            full((2304, 256), BF16),
            full((2304, 256), BF16),
        ),
        scratch_shapes=[pltpu.VMEM((432, 256), F32), pltpu.VMEM((1728, 256), F32)],
        compiler_params=PARAMS,
    )(k1, k2, k3, k4)


def fold(row, width):
    total = row[:, 0:128]
    for j in range(1, row.shape[1] // 128):
        total = total + row[:, j * 128 : (j + 1) * 128]
    step = 64
    while step >= width:
        total = total + pltpu.roll(total, step, 1)
        step //= 2
    return total


def pack_stats(s1, s2, width):
    return jnp.where(iota((1, 128), 1) < 64, fold(s1, width), fold(s2, width))


def unpack_stats(total, cells):
    low = iota((1, 128), 1) < 64
    other = pltpu.roll(total, 64, 1)
    mean = jnp.where(low, total, other) / cells
    variance = jnp.where(low, other, total) / cells - mean * mean
    return mean, variance


def paired_rows(ref, j, count):
    return jnp.concatenate(
        [
            jnp.maximum(ref[k, pl.ds(0, count, stride=2), :], ref[k, pl.ds(1, count, stride=2), :])
            for k in (j, j + 1)
        ],
        axis=1,
    )


def first_kernel(lo_ref, mid_ref, hi_ref, w1_ref, lhs_ref, stats_ref):
    lane = iota((48, 128), 1)

    def windows(piece_ref, base, first, count):
        def step(i, carry):
            v = piece_ref[first + i].astype(F32)
            for q in range(3):
                start = 119 + 48 * q
                a, b = start // 128, (start + 49) // 128 + 1
                src = v[:, a * 128 : b * 128]
                width = (b - a) * 128
                wa = pltpu.roll(src, width - (start - a * 128), 1)[:, 0:128]
                wb = pltpu.roll(wa, 64, 1)
                left = jnp.where(lane < 64, pltpu.roll(wa, 1, 0), wb)
                right = pltpu.roll(wa, 47, 0)
                lhs_ref[q, base + i, :, 0:128] = left.astype(BF16)
                lhs_ref[q, base + i, :, 128:256] = right.astype(BF16)
            return carry

        lax.fori_loop(0, count, step, 0)

    windows(lo_ref, 0, 1, 7)
    windows(mid_ref, 7, 0, 8)
    windows(hi_ref, 15, 0, 7)
    s1 = jnp.zeros((1, 768), F32)
    s2 = jnp.zeros((1, 768), F32)
    for q in range(3):
        lhs = jnp.concatenate([lhs_ref[q, 6 + dx : 14 + dx, :, :] for dx in range(3)], axis=2)
        lhs = lhs.reshape(8 * 48, 768)
        r = jnp.dot(lhs, w1_ref[...], preferred_element_type=F32)
        own = r.reshape(8, 48, 768)[:, 8:40, :].reshape(256, 768)
        row1 = jnp.sum(own, axis=0, keepdims=True)
        row2 = jnp.sum(own * own, axis=0, keepdims=True)
        at = iota((1, 768), 1)
        if q == 0:
            row1, row2 = (jnp.where(at >= 128, r_, 0.0) for r_ in (row1, row2))
        if q == 2:
            row1, row2 = (jnp.where(at < 640, r_, 0.0) for r_ in (row1, row2))
        s1, s2 = s1 + row1, s2 + row2
    stats_ref[...] = jnp.broadcast_to(pack_stats(s1, s2, 16).reshape(1, 1, 128), (DEVICES, 1, 128))


def first_part(lo, mid, hi, w1):
    return pl.pallas_call(
        first_kernel,
        out_shape=(full((3, 22, 48, 256), BF16), full((DEVICES, 1, 128), F32)),
        compiler_params=PARAMS,
    )(lo, mid, hi, w1)


def second_kernel(
    at_ref, lhs_ref, stats_ref, gain_ref, shift_ref, w1_ref, w2_ref, f1_ref, r2_ref, out_stats_ref, half, p1, pd
):
    mean, variance = unpack_stats(jnp.sum(stats_ref[...], axis=0), VOXELS_1)
    factor = gain_ref[...] * lax.rsqrt(variance + EPSILON)
    shift = shift_ref[...]
    mean, factor, shift = (jnp.concatenate([v] * 6, axis=1) for v in (mean, factor, shift))
    row, col = iota((256, 256), 0), iota((256, 256), 1)
    pick = (row == (col % 128) // 16 * 32 + col % 16 + col // 128 * 16).astype(BF16)
    bx, by, bz = at_ref[0], at_ref[1], at_ref[2]
    p1[:, :, 1152:1280] = jnp.zeros((10, 24, 128), F32)
    for q in range(3):
        lhs = jnp.concatenate([lhs_ref[q, dx : 20 + dx, :, :] for dx in range(3)], axis=2)
        r = jnp.dot(lhs.reshape(960, 768), w1_ref[...], preferred_element_type=F32)
        f = jnp.maximum((r - mean) * factor + shift, 0.0)
        f = f.reshape(20, 48, 768)
        a, b = (128 if q == 0 else 0), (640 if q == 2 else 768)
        f1_ref[:, :, q * 768 - 128 + a : q * 768 - 128 + b] = f[6:14, 8:40, a:b].astype(BF16)
        pairs = jnp.max(f.reshape(10, 2, 48, 768), axis=1).reshape(480, 768)
        for j in range(6):
            half[j] = pairs[:, j * 128 : (j + 1) * 128]
        for j in range(3):
            g = paired_rows(half, 2 * j, 240)
            both = jnp.dot(g.astype(BF16), pick, preferred_element_type=F32)
            pooled = jnp.maximum(both[:, 0:128], both[:, 128:256])
            at = q * 384 + j * 128
            p1[:, :, at : at + 128] = pooled.reshape(10, 24, 128)
    gy = iota((24, 1280), 0) - 4 + by * 16
    gz = iota((24, 1280), 1) // 16 - 4 + bz * 64
    inside = (gy >= 0) & (gy < 64) & (gz >= 0) & (gz < 256)

    def mask(i, carry):
        gx = i - 3 + bx * 4
        v = jnp.where(inside & (gx >= 0) & (gx < 32), p1[i], 0.0)
        pd[0, i] = pltpu.roll(v, 1, 0).astype(BF16)
        pd[1, i] = v.astype(BF16)
        pd[2, i] = pltpu.roll(v, 23, 0).astype(BF16)
        return carry

    lax.fori_loop(0, 10, mask, 0)
    s1 = jnp.zeros((1, 256), F32)
    s2 = jnp.zeros((1, 256), F32)
    lane = iota((1, 256), 1)
    for t in range(9):
        lanes = slice(128 * t, 128 * t + 256)
        lhs = jnp.concatenate(
            [pd[dy, dx : dx + 8, :, lanes].astype(F32).reshape(192, 256).astype(BF16) for dx in range(3) for dy in range(3)], axis=1
        )
        r = jnp.dot(lhs, w2_ref[...], preferred_element_type=F32).reshape(8, 24, 256)
        r2_ref[:, :, t * 256 : (t + 1) * 256] = r
        own = r[2:6, 4:20, :]
        row1 = jnp.sum(jnp.sum(own, axis=0), axis=0, keepdims=True)
        row2 = jnp.sum(jnp.sum(own * own, axis=0), axis=0, keepdims=True)
        if t == 0:
            row1, row2 = (jnp.where(lane >= 64, r_, 0.0) for r_ in (row1, row2))
        if t == 8:
            row1, row2 = (jnp.where(lane < 64, r_, 0.0) for r_ in (row1, row2))
        s1, s2 = s1 + row1, s2 + row2
    out_stats_ref[...] = jnp.broadcast_to(pack_stats(s1, s2, 32).reshape(1, 1, 128), (DEVICES, 1, 128))


def second_part(at, lhs, stats, gain, shift, w1, w2):
    vmem = pl.BlockSpec(memory_space=pltpu.VMEM)
    return pl.pallas_call(
        second_kernel,
        in_specs=[pl.BlockSpec(memory_space=pltpu.SMEM)] + [vmem] * 6,
        out_specs=(vmem, vmem, vmem),
        out_shape=(
            full((8, 32, 2048), BF16),
            full((8, 24, 2304), F32),
            full((DEVICES, 1, 128), F32),
        ),
        scratch_shapes=[
            pltpu.VMEM((6, 480, 128), F32),
            pltpu.VMEM((10, 24, 1280), F32),
            pltpu.VMEM((3, 10, 24, 1280), BF16),
        ],
        compiler_params=PARAMS,
    )(at, lhs, stats, gain, shift, w1, w2)


def third_kernel(at_ref, r2_ref, stats_ref, gain_ref, shift_ref, w3_ref, f2_ref, r3_ref, out_ref, half, own2, p2, yrow):
    mean, variance = unpack_stats(jnp.sum(stats_ref[...], axis=0), VOXELS_1 / 8)
    factor = gain_ref[...] * lax.rsqrt(variance + EPSILON)
    shift = shift_ref[...]
    mean, factor, shift = (jnp.concatenate([v] * 18, axis=1) for v in (mean, factor, shift))
    bx, by, bz = at_ref[0], at_ref[1], at_ref[2]
    row, col = iota((256, 256), 0), iota((256, 256), 1)
    pick = (row == (col % 128) // 32 * 64 + col % 32 + col // 128 * 32).astype(BF16)
    for px in range(4):
        fs = []
        for i in range(2):
            f = jnp.maximum((r2_ref[2 * px + i] - mean) * factor + shift, 0.0)
            fs.append(f)
            if px in (1, 2):
                own2[...] = pltpu.roll(f, 2304 - 64, 1)[:, 0:2048]
                f2_ref[2 * (px - 1) + i] = own2[4:20, :].astype(BF16)
        pairs = jnp.maximum(fs[0], fs[1])
        for j in range(18):
            half[j, px * 24 : px * 24 + 24, :] = pairs[:, j * 128 : (j + 1) * 128]
    gy = iota((12, 128), 0) - 2 + by * 8
    for j in range(9):
        g = paired_rows(half, 2 * j, 48)
        both = jnp.dot(g.astype(BF16), pick, preferred_element_type=F32)
        pooled = jnp.maximum(both[:, 0:128], both[:, 128:256])
        gz = iota((12, 128), 1) // 32 + 4 * j - 1 + bz * 32
        inside = (gy >= 0) & (gy < 32) & (gz >= 0) & (gz < 128)
        for px in range(4):
            gx = px - 1 + bx * 2
            p2[px, 0:12, j * 128 : (j + 1) * 128] = jnp.where(
                inside & (gx >= 0) & (gx < 16), pooled[px * 12 : px * 12 + 12, :], 0.0
            )
    planes = []
    for dx in range(3):
        for dy in range(3):
            pieces = []
            for t in range(8):
                for x in range(2):
                    pieces.append(p2[x + dx, 1 + dy : 9 + dy, 128 * t : 128 * t + 256])
            planes.append(jnp.concatenate(pieces, axis=0).astype(BF16))
    r = jnp.dot(jnp.concatenate(planes, axis=1), w3_ref[...], preferred_element_type=F32)
    r3_ref[...] = r
    s1 = fold(jnp.sum(r, axis=0, keepdims=True), 64)
    s2 = fold(jnp.sum(r * r, axis=0, keepdims=True), 64)
    low = iota((8, 128), 1) < 64
    for t in range(8):
        m = jnp.maximum(r[t * 16 : t * 16 + 8, :], r[t * 16 + 8 : t * 16 + 16, :])
        a, b = m[:, 0:128], m[:, 128:256]
        a = jnp.maximum(a, pltpu.roll(a, 64, 1))
        b = jnp.maximum(b, pltpu.roll(b, 64, 1))
        yrow[:, t * 128 : (t + 1) * 128] = jnp.where(low, a, b)
    pooled = jnp.concatenate([jnp.maximum(yrow[2 * i : 2 * i + 1, :], yrow[2 * i + 1 : 2 * i + 2, :]) for i in range(4)], axis=0)
    wide = pltpu.roll(jnp.concatenate([pooled, jnp.zeros((4, 128), F32)], axis=1), 64, 1)
    lane = iota((4, 1152), 1)
    wide = jnp.where(lane < 64, jnp.concatenate([s1] * 9, axis=1), wide)
    wide = jnp.where(lane >= 1088, jnp.concatenate([s2] * 9, axis=1), wide)
    out_ref[...] = jnp.broadcast_to(wide.reshape(1, 4, 1152), (DEVICES, 4, 1152))


def third_part(at, r2, stats, gain, shift, w3):
    vmem = pl.BlockSpec(memory_space=pltpu.VMEM)
    return pl.pallas_call(
        third_kernel,
        in_specs=[pl.BlockSpec(memory_space=pltpu.SMEM)] + [vmem] * 5,
        out_specs=(vmem, vmem, vmem),
        out_shape=(
            full((4, 16, 2048), BF16),
            full((128, 256), F32),
            full((DEVICES, 4, 1152), F32),
        ),
        scratch_shapes=[
            pltpu.VMEM((18, 96, 128), F32),
            pltpu.VMEM((24, 2048), F32),
            pltpu.VMEM((4, 16, 1152), F32),
            pltpu.VMEM((8, 1024), F32),
        ],
        compiler_params=PARAMS,
    )(at, r2, stats, gain, shift, w3)


def fourth_kernel(r3_ref, all_ref, gain3_ref, shift3_ref, w4_ref, gain4_ref, shift4_ref, f3_ref, out_ref, p3, pd, r4):
    edge = jnp.sum(all_ref[:, :, 0:128], axis=0)[0:1, :]
    tail = jnp.sum(all_ref[:, :, 1024:1152], axis=0)[0:1, :]
    mean, variance = unpack_stats(jnp.where(iota((1, 128), 1) < 64, edge, tail), VOXELS_1 / 64)
    factor = gain3_ref[...] * lax.rsqrt(variance + EPSILON)
    shift = shift3_ref[...]
    mean2, factor2, shift2 = (jnp.concatenate([v] * 2, axis=1) for v in (mean, factor, shift))
    f3 = jnp.maximum((r3_ref[...] - mean2) * factor2 + shift2, 0.0)
    for t in range(8):
        for x in range(2):
            f3_ref[x, :, t * 256 : (t + 1) * 256] = f3[t * 16 + x * 8 : t * 16 + x * 8 + 8, :].astype(BF16)
    mean9, factor9, shift9 = (jnp.concatenate([v] * 9, axis=1) for v in (mean, factor, shift))
    lane = iota((4, 128), 1)
    zero = jnp.zeros((16, 4224), BF16)
    for dy in range(3):
        pd[dy, 0] = zero
        pd[dy, 9] = zero

    def place(gx, carry):
        for gy in range(4):
            last = jnp.zeros((4, 128), F32)
            for gz in range(4):
                v = jnp.maximum((all_ref[gx * 16 + gy * 4 + gz] - mean9) * factor9 + shift9, 0.0)
                start = gz * 1024
                p3[4 * gy : 4 * gy + 4, start : start + 128] = jnp.where(lane < 64, last, v[:, 0:128])
                p3[4 * gy : 4 * gy + 4, start + 128 : start + 1024] = v[:, 128:1024]
                last = v[:, 1024:1152]
            p3[4 * gy : 4 * gy + 4, 4096:4224] = jnp.where(lane < 64, last, 0.0)
        v = p3[...]
        y = iota((16, 4224), 0)
        pd[0, gx + 1] = jnp.where(y > 0, pltpu.roll(v, 1, 0), 0.0).astype(BF16)
        pd[1, gx + 1] = v.astype(BF16)
        pd[2, gx + 1] = jnp.where(y < 15, pltpu.roll(v, 15, 0), 0.0).astype(BF16)
        return carry

    lax.fori_loop(0, 8, place, 0)

    def tile(t, carry):
        s1, s2 = carry
        lanes = pl.ds(pl.multiple_of(128 * t, 128), 256)
        lhs = jnp.concatenate(
            [pd[dy, dx : dx + 8, :, lanes].reshape(128, 256) for dx in range(3) for dy in range(3)], axis=1
        )
        r = jnp.dot(lhs, w4_ref[...], preferred_element_type=F32)
        r4[t] = r
        return s1 + jnp.sum(r, axis=0, keepdims=True), s2 + jnp.sum(r * r, axis=0, keepdims=True)

    zeros = jnp.zeros((1, 256), F32)
    s1, s2 = lax.fori_loop(0, 32, tile, (zeros, zeros))
    cells = VOXELS_1 / 512
    mean = fold(s1, 128) / cells
    variance = fold(s2, 128) / cells - mean * mean
    factor = gain4_ref[...] * lax.rsqrt(variance + EPSILON)
    mean, factor, shift = (jnp.concatenate([v] * 2, axis=1) for v in (mean, factor, shift4_ref[...]))

    def finish(t, carry):
        f = jnp.maximum((r4[t] - mean) * factor + shift, 0.0).astype(BF16)
        out_ref[:, :, pl.ds(pl.multiple_of(256 * t, 256), 256)] = f.reshape(8, 16, 256)
        return carry

    lax.fori_loop(0, 32, finish, 0)


def fourth_part(r3, everything, gain3, shift3, w4, gain4, shift4):
    return pl.pallas_call(
        fourth_kernel,
        out_shape=(full((2, 8, 2048), BF16), full((8, 16, 8192), BF16)),
        scratch_shapes=[
            pltpu.VMEM((16, 4224), F32),
            pltpu.VMEM((3, 10, 16, 4224), BF16),
            pltpu.VMEM((32, 128, 256), F32),
        ],
        compiler_params=PARAMS,
    )(r3, everything, gain3, shift3, w4, gain4, shift4)


def neighbours(low_face, high_face, axis):
    count = lax.axis_size(axis)
    up = [(i, i + 1) for i in range(count - 1)]
    down = [(i + 1, i) for i in range(count - 1)]
    return lax.ppermute(high_face, axis, up), lax.ppermute(low_face, axis, down)


def along(vector, lanes):
    return jnp.tile(vector, lanes // vector.shape[0]).reshape(1, lanes)


def shards(volume, k1, g1, b1, k2, g2, b2, k3, g3, b3, k4, g4, b4):
    at = jnp.stack([lax.axis_index(a) for a in AXES]).astype(jnp.int32)
    w1, w2, w3, w4 = bands(k1.reshape(27, 16), k2.reshape(432, 32), k3.reshape(864, 64), k4.reshape(1728, 128))
    low, high = neighbours(volume, volume, "gz")
    wide = jnp.concatenate([low, volume, high], axis=2)
    low, high = neighbours(wide[:, 0:8, :], wide[:, 24:32, :], "gy")
    mid = jnp.concatenate([low, wide, high], axis=1)
    low, high = neighbours(mid, mid, "gx")
    lhs, stats = first_part(low, mid, high, w1)
    stats = lax.all_to_all(stats, AXES, 0, 0, tiled=True)
    f1, r2, stats = second_part(at, lhs, stats, along(g1, 128), along(b1, 128), w1, w2)
    stats = lax.all_to_all(stats, AXES, 0, 0, tiled=True)
    f2, r3, packed = third_part(at, r2, stats, along(g2, 128), along(b2, 128), w3)
    everything = lax.all_to_all(packed, AXES, 0, 0, tiled=True)
    f3, f4 = fourth_part(r3, everything, along(g3, 128), along(b3, 128), w4, along(g4, 128), along(b4, 128))
    return f1, f2, f3, f4


def solution(mesh):
    spread = P("gx", "gy", "gz")
    return jax.shard_map(
        shards,
        mesh=mesh,
        in_specs=(spread,) + (P(),) * 12,
        out_specs=(spread, spread, spread, P()),
        check_vma=False,
    )
```

```python
import functools

import jax
import jax.numpy as jnp
from jax import lax
from jax.experimental import pallas as pl
from jax.experimental.pallas import tpu as pltpu
from jax.sharding import Mesh
from jax.sharding import PartitionSpec as P

EPSILON = 1e-05
F32 = jnp.float32
BF16 = jnp.bfloat16
AXES = ("gx", "gh", "gc", "gz")
CHIPS = ("gx", "gh", "gz")
DEVICES = 128
VOXELS_1 = 64.0 * 128.0 * 512.0
PARAMS = pltpu.CompilerParams(vmem_limit_bytes=40 * 1024 * 1024)


def full(shape, dtype):
    return jax.ShapeDtypeStruct(shape, dtype)


def iota(shape, dim):
    return lax.broadcasted_iota(jnp.int32, shape, dim)


VMEM = pl.BlockSpec(memory_space=pltpu.VMEM)
ANY = pl.BlockSpec(memory_space=pl.ANY)


def near(shape, dtype):
    return pltpu.VMEM(shape, dtype)


def far(shape, dtype):
    return pltpu.HBM(shape, dtype)


def held(array):
    return pltpu.with_memory_space_constraint(array, pltpu.HBM)


def call(kernel, outs, ins, scratch=()):
    return pl.pallas_call(
        kernel,
        in_specs=[spec for _, spec in ins],
        out_specs=tuple(VMEM for _ in outs),
        out_shape=tuple(outs),
        scratch_shapes=[s if not isinstance(s, tuple) else pltpu.VMEM(*s) for s in scratch],
        compiler_params=PARAMS,
    )(*[array for array, _ in ins])


def position():
    gx, gh, gc, gz = (lax.axis_index(a) for a in AXES)
    return gx, gh * 2 + gc, gz


def first_band_kernel(k_ref, w_ref, far_ref):
    spread = (iota((16, 768), 1) % 16 == iota((16, 768), 0)).astype(BF16)
    taps = jnp.dot(k_ref[...], spread, preferred_element_type=F32)
    lag = iota((64, 768), 0) - iota((64, 768), 1) // 16
    for dx in range(3):
        for dy in range(3):
            block = jnp.zeros((64, 768), F32)
            for dz in range(3):
                t = (dx * 3 + dy) * 3 + dz
                block = jnp.where(lag == dz, taps[t : t + 1, :], block)
            w_ref[dx * 256 + dy * 64 : dx * 256 + dy * 64 + 64, :] = block.astype(BF16)
        w_ref[dx * 256 + 192 : dx * 256 + 256, :] = jnp.zeros((64, 768), BF16)
    far_ref[...] = w_ref[...]


def first_band(k):
    return call(first_band_kernel, [near((768, 768), BF16), far((768, 768), BF16)], [(k, VMEM)])


def params_kernel(*refs):
    ins, out_ref, local, sem = refs[:8], refs[8], refs[9:17], refs[17]
    copies = [pltpu.make_async_copy(a, b, sem.at[i]) for i, (a, b) in enumerate(zip(ins, local))]
    for c in copies:
        c.start()
    for c in copies:
        c.wait()
    lane = iota((1, 128), 1)
    for i, ref in enumerate(local):
        count = ref.shape[0]
        row = jnp.zeros((1, 128), F32)
        for c in range(count):
            row = jnp.where(lane % count == c, ref[c], row)
        out_ref[i : i + 1, :] = row


def params(*vectors):
    return call(
        params_kernel,
        [near((8, 128), F32)],
        [(held(v), ANY) for v in vectors],
        [pltpu.SMEM(v.shape, F32) for v in vectors] + [pltpu.SemaphoreType.DMA((8,))],
    )[0]


def band_kernel(cin, cout, first, k_ref, w_ref, t_ref):
    outs = 256 // cout
    tile = (iota((cout, 256), 1) % cout == iota((cout, 256), 0)).astype(BF16)
    t_ref[...] = jnp.dot(k_ref[...], tile, preferred_element_type=F32)
    zo = iota((cin, 256), 1) // cout

    def plane(p, carry):
        for zi in range(-first, 256 // cin - first):
            block = jnp.zeros((cin, 256), F32)
            if 0 <= zi < outs + 2:
                for dz in range(3):
                    start = pl.multiple_of((p * 3 + dz) * cin, cin)
                    block = jnp.where(zo == zi - dz, t_ref[pl.ds(start, cin), :], block)
            start = pl.multiple_of(p * 256 + (zi + first) * cin, cin)
            w_ref[pl.ds(start, cin), :] = block.astype(BF16)
        return carry

    lax.fori_loop(0, 9, plane, 0)


def band(k, first):
    cin, cout = k.shape[3:]
    return call(
        functools.partial(band_kernel, cin, cout, first),
        [near((2304, 256), BF16)],
        [(held(k.reshape(27 * cin, cout)), VMEM)],
        [((27 * cin, 256), F32)],
    )[0]


def fold(row, width):
    total = row[:, 0:128]
    for j in range(1, row.shape[1] // 128):
        total = total + row[:, j * 128 : (j + 1) * 128]
    step = 64
    while step >= width:
        total = total + pltpu.roll(total, step, 1)
        step //= 2
    return total


def pack_stats(s1, s2, width):
    return jnp.where(iota((1, 128), 1) < 64, fold(s1, width), fold(s2, width))


def normaliser(total, cells, params_ref, level, copies):
    lane = iota((1, 128), 1)
    other = pltpu.roll(total, 64, 1)
    mean = jnp.where(lane < 64, total, other) / cells
    variance = jnp.where(lane < 64, other, total) / cells - mean * mean
    shift = params_ref[2 * level + 1 : 2 * level + 2, :]
    factor = params_ref[2 * level : 2 * level + 1, :] * lax.rsqrt(variance + EPSILON)
    return tuple(jnp.concatenate([v] * copies, axis=1) for v in (mean, factor, shift))


def settle(response, normal):
    mean, factor, shift = normal
    return jnp.maximum((response - mean) * factor + shift, 0.0)


def slots(stats):
    return jnp.broadcast_to(stats.reshape(1, 1, 128), (DEVICES, 1, 128))


def paired_rows(ref, j, count):
    return jnp.maximum(ref[j, pl.ds(0, count, stride=2), :], ref[j, pl.ds(1, count, stride=2), :])


def fill(out_ref, at, v):
    lane = iota((48, 128), 1)
    for q, part, turn in ((0, v, 9), (1, v[:, 0:128], 128 - 39), (2, v, 256 - 87)):
        wa = pltpu.roll(part, turn, 1)[:, 0:128]
        wb = pltpu.roll(wa, 64, 1)
        out_ref[q, at, :, 0:128] = jnp.where(lane < 64, pltpu.roll(wa, 1, 0), wb).astype(BF16)
        out_ref[q, at, :, 128:256] = pltpu.roll(wa, 47, 0).astype(BF16)


def response_1(planes, w1_ref):
    lhs = jnp.concatenate(planes, axis=2)
    n, rows, _ = lhs.shape
    r = jnp.dot(lhs.reshape(n * rows, 768), w1_ref[...], preferred_element_type=F32)
    return r.reshape(n, rows, 768)


def sums_1(r, q):
    own = r[:, 8:40, :].reshape(-1, 768)
    row1 = jnp.sum(own, axis=0, keepdims=True)
    row2 = jnp.sum(own * own, axis=0, keepdims=True)
    at = iota((1, 768), 1)
    if q == 0:
        row1, row2 = (jnp.where(at >= 128, r_, 0.0) for r_ in (row1, row2))
    if q == 2:
        row1, row2 = (jnp.where(at < 640, r_, 0.0) for r_ in (row1, row2))
    return row1, row2


def halve_rows(r, rows, half_ref, q):
    n = r.shape[0]
    flat = r.reshape(n * 48, 768)
    for j in range(6):
        rows[j, 0 : n * 48] = flat[:, j * 128 : (j + 1) * 128]
    for j in range(6):
        half_ref[q * 6 + j] = paired_rows(rows, j, n * 24)


def middle_kernel(mid_ref, w1_ref, lhs_ref, far_ref, half_ref, sums_ref, rows):
    def step(i, carry):
        fill(lhs_ref, i, mid_ref[i].astype(F32))
        return carry

    lax.fori_loop(0, 8, step, 0, unroll=4)
    s1 = jnp.zeros((1, 768), F32)
    s2 = jnp.zeros((1, 768), F32)
    for q in range(3):
        r = response_1([lhs_ref[q, dx : 6 + dx] for dx in range(3)], w1_ref)
        row1, row2 = sums_1(r, q)
        s1, s2 = s1 + row1, s2 + row2
        halve_rows(r, rows, half_ref, q)
    sums_ref[0:1, :] = s1
    sums_ref[1:2, :] = s2
    far_ref[...] = lhs_ref[...]


def middle_part(mid, w1):
    return call(
        middle_kernel,
        [near((3, 8, 48, 256), BF16), far((3, 8, 48, 256), BF16), far((18, 144, 128), F32), near((8, 768), F32)],
        [(mid, VMEM), (w1, VMEM)],
        [((6, 288, 128), F32)],
    )


def first_kernel(lo_ref, hi_ref, mid_ref, sums_ref, w1_ref, ends_ref, half_ref, stats_ref, rows, lo, hi, sems):
    copies = [
        pltpu.make_async_copy(lo_ref.at[7], lo, sems.at[0]),
        pltpu.make_async_copy(hi_ref.at[0], hi, sems.at[1]),
    ]
    for c in copies:
        c.start()
    ends_ref[:, 1:2] = mid_ref[:, 0:1]
    ends_ref[:, 2:3] = mid_ref[:, 7:8]
    for c in copies:
        c.wait()
    fill(ends_ref, 0, lo[...].astype(F32))
    fill(ends_ref, 3, hi[...].astype(F32))
    planes = []
    for q in range(3):
        a = [ends_ref[q, 0:1], mid_ref[q, 0:1], mid_ref[q, 1:2]]
        b = [mid_ref[q, 6:7], mid_ref[q, 7:8], ends_ref[q, 3:4]]
        planes.append([jnp.concatenate([a[dx], b[dx]], axis=0) for dx in range(3)])
    r = response_1([jnp.concatenate([planes[q][dx] for q in range(3)], axis=0) for dx in range(3)], w1_ref)
    s1 = sums_ref[0:1, :]
    s2 = sums_ref[1:2, :]
    for q in range(3):
        row1, row2 = sums_1(r[2 * q : 2 * q + 2], q)
        s1, s2 = s1 + row1, s2 + row2
    stats_ref[...] = slots(pack_stats(s1, s2, 16))
    for q in range(3):
        halve_rows(r[2 * q : 2 * q + 2], rows, half_ref, q)


def first_part(lo, hi, lhs_mid, sums, w1):
    return call(
        first_kernel,
        [far((3, 4, 48, 256), BF16), far((18, 48, 128), F32), far((DEVICES, 1, 128), F32)],
        [(held(lo), ANY), (held(hi), ANY), (lhs_mid, VMEM), (sums, VMEM), (w1, VMEM)],
        [((6, 96, 128), F32), ((48, 256), BF16), ((48, 256), BF16), pltpu.SemaphoreType.DMA((2,))],
    )


def wide_first_kernel(
    lo_ref, hi_ref, ends_ref, half_mid_ref, half_edge_ref, w1_far, half_ref, lhs, rows, wide, w1_ref, sem
):
    weights = pltpu.make_async_copy(w1_far, w1_ref, sem)
    weights.start()

    def step(i, carry):
        fill(lhs, i, lo_ref[1 + i].astype(F32))
        fill(lhs, 10 + i, hi_ref[1 + i].astype(F32))
        return carry

    lax.fori_loop(0, 6, step, 0, unroll=2)
    lhs[:, 6:10] = ends_ref[...]
    weights.wait()
    for q in range(3):
        planes = [jnp.concatenate([lhs[q, dx : 6 + dx], lhs[q, 8 + dx : 14 + dx]], axis=0) for dx in range(3)]
        halve_rows(response_1(planes, w1_ref), rows, wide, q)

    def merge(j, carry):
        outer = wide[j].reshape(6, 2, 24, 128)
        inner = half_mid_ref[j].reshape(6, 24, 128)
        edges = half_edge_ref[j].reshape(2, 24, 128)
        outer = jnp.maximum(outer[:, 0], outer[:, 1])
        half_ref[j, 0:72] = outer[0:3].reshape(72, 128)
        half_ref[j, 72:96] = jnp.maximum(edges[0], inner[0])
        half_ref[j, 96:120] = jnp.maximum(inner[1], inner[2])
        half_ref[j, 120:144] = jnp.maximum(inner[3], inner[4])
        half_ref[j, 144:168] = jnp.maximum(inner[5], edges[1])
        half_ref[j, 168:240] = outer[3:6].reshape(72, 128)
        return carry

    lax.fori_loop(0, 18, merge, 0)


def wide_first_part(lo, hi, ends, half_mid, half_edge, w1):
    return call(
        wide_first_kernel,
        [near((18, 240, 128), F32)],
        [(held(a), VMEM) for a in (lo, hi, ends, half_mid, half_edge)] + [(held(w1), ANY)],
        [((3, 16, 48, 256), BF16), ((6, 576, 128), F32), ((18, 288, 128), F32), ((768, 768), BF16)]
        + [pltpu.SemaphoreType.DMA(())],
    )[0]


def first_output_kernel(mid_ref, ends_ref, w1_ref, stats_ref, params_ref, f1_ref):
    normal = normaliser(jnp.sum(stats_ref[...], axis=0), VOXELS_1, params_ref, 0, 6)
    for q in range(3):
        middle = mid_ref[q]
        planes = [
            jnp.concatenate([ends_ref[q, 0:1], middle[0:7]], axis=0),
            middle,
            jnp.concatenate([middle[1:8], ends_ref[q, 3:4]], axis=0),
        ]
        f = settle(response_1([p[:, 8:40, :] for p in planes], w1_ref), normal)
        a, b = (128 if q == 0 else 0), (640 if q == 2 else 768)
        f1_ref[:, :, q * 768 - 128 + a : q * 768 - 128 + b] = f[:, :, a:b].astype(BF16)


def first_output(lhs_mid, ends, w1, stats, table):
    return call(
        first_output_kernel,
        [full((8, 32, 2048), BF16)],
        [(held(a), VMEM) for a in (lhs_mid, ends, w1)] + [(stats, VMEM), (table, VMEM)],
    )[0]


def selector(chans):
    row, col = iota((256, 256), 0), iota((256, 256), 1)
    return (row == (col % 128) // chans * (2 * chans) + col % chans + col // 128 * chans).astype(BF16)


def halved(left, right, normal, pick):
    features = jnp.concatenate([settle(left, normal), settle(right, normal)], axis=1).astype(BF16)
    both = jnp.dot(features, pick, preferred_element_type=F32)
    return jnp.maximum(both[:, 0:128], both[:, 128:256])


def second_kernel(half_ref, stats_ref, params_ref, w2_ref, p1_ref, r2_ref, out_stats_ref, p1, pd):
    normal = normaliser(jnp.sum(stats_ref[...], axis=0), VOXELS_1, params_ref, 0, 1)
    pick = selector(16)
    bx, by, bz = position()
    p1[:, :, 1152:1280] = jnp.zeros((10, 24, 128), F32)
    gy = iota((10, 24, 128), 1) - 4 + by * 16
    gx = iota((10, 24, 128), 0) - 3 + bx * 4
    inside = (gy >= 0) & (gy < 64) & (gx >= 0) & (gx < 32)
    for j in range(9):
        pooled = halved(half_ref[2 * j], half_ref[2 * j + 1], normal, pick).reshape(10, 24, 128)
        gz = iota((10, 24, 128), 2) // 16 - 4 + 8 * j + bz * 64
        p1[:, :, j * 128 : (j + 1) * 128] = jnp.where(inside & (gz >= 0) & (gz < 256), pooled, 0.0)
    for dy in range(3):
        pd[dy] = p1[2:8, 3 + dy : 19 + dy, :].astype(BF16)
    p1_ref[...] = p1[...].astype(BF16)
    planes = []
    for dx in range(3):
        for dy in range(3):
            pieces = [pd[dy, dx : dx + 4, :, 128 * t : 128 * t + 256].reshape(64, 256) for t in range(9)]
            planes.append(jnp.concatenate(pieces, axis=0))
    r = jnp.dot(jnp.concatenate(planes, axis=1), w2_ref[...], preferred_element_type=F32)
    r2_ref[...] = r
    s1 = jnp.zeros((1, 256), F32)
    s2 = jnp.zeros((1, 256), F32)
    lane = iota((1, 256), 1)
    for t in range(9):
        own = r[64 * t : 64 * t + 64]
        row1 = jnp.sum(own, axis=0, keepdims=True)
        row2 = jnp.sum(own * own, axis=0, keepdims=True)
        if t == 0:
            row1, row2 = (jnp.where(lane >= 64, r_, 0.0) for r_ in (row1, row2))
        if t == 8:
            row1, row2 = (jnp.where(lane < 64, r_, 0.0) for r_ in (row1, row2))
        s1, s2 = s1 + row1, s2 + row2
    out_stats_ref[...] = slots(pack_stats(s1, s2, 32))


def second_part(half, stats, table, w2):
    return call(
        second_kernel,
        [far((10, 24, 1280), BF16), far((576, 256), F32), far((DEVICES, 1, 128), F32)],
        [(a, VMEM) for a in (half, stats, table, w2)],
        [((10, 24, 1280), F32), ((3, 6, 16, 1280), BF16)],
    )


def wide_second_kernel(p1_ref, w2_ref, half_ref, pd, rows):
    def shift(i, carry):
        v = p1_ref[i].astype(F32)
        pd[0, i] = pltpu.roll(v, 1, 0)
        pd[1, i] = v
        pd[2, i] = pltpu.roll(v, 23, 0)
        return carry

    lax.fori_loop(0, 10, shift, 0)
    for t in range(0, 9, 3):
        planes = []
        for dx in range(3):
            for dy in range(3):
                pieces = [pd[dy, dx : dx + 8, :, 128 * u : 128 * u + 256].reshape(192, 256) for u in range(t, t + 3)]
                planes.append(jnp.concatenate(pieces, axis=0).astype(BF16))
        r = jnp.dot(jnp.concatenate(planes, axis=1), w2_ref[...], preferred_element_type=F32)
        r = jnp.max(r.reshape(3, 4, 2, 24, 256), axis=2).reshape(3, 96, 256)
        for i in range(3):
            for j in range(2):
                rows[2 * i + j] = r[i, :, j * 128 : (j + 1) * 128]
        for j in range(6):
            half_ref[2 * t + j] = paired_rows(rows, j, 48)


def wide_second_part(p1, w2):
    return call(
        wide_second_kernel,
        [near((18, 48, 128), F32)],
        [(held(p1), VMEM), (w2, VMEM)],
        [((3, 10, 24, 1280), F32), ((6, 96, 128), F32)],
    )[0]


def second_output_kernel(r2_ref, stats_ref, params_ref, f2_ref):
    normal = normaliser(jnp.sum(stats_ref[...], axis=0), VOXELS_1 / 8, params_ref, 1, 2)
    f = [settle(r2_ref[64 * t : 64 * t + 64, :], normal) for t in range(9)]
    wide = pltpu.roll(jnp.concatenate(f, axis=1), 2304 - 64, 1)[:, 0:2048]
    f2_ref[...] = wide.reshape(4, 16, 2048).astype(BF16)


def second_output(r2, stats, table):
    return call(
        second_output_kernel,
        [full((4, 16, 2048), BF16)],
        [(held(r2), VMEM), (stats, VMEM), (table, VMEM)],
    )[0]


def third_kernel(half_ref, stats_ref, params_ref, w3_ref, r3_ref, out_ref, p2, yrow):
    normal = normaliser(jnp.sum(stats_ref[...], axis=0), VOXELS_1 / 8, params_ref, 1, 1)
    bx, by, bz = position()
    pick = selector(32)
    gy = iota((12, 128), 0) - 2 + by * 8
    for j in range(9):
        pooled = halved(half_ref[2 * j], half_ref[2 * j + 1], normal, pick)
        gz = iota((12, 128), 1) // 32 + 4 * j - 1 + bz * 32
        inside = (gy >= 0) & (gy < 32) & (gz >= 0) & (gz < 128)
        for px in range(4):
            gx = px - 1 + bx * 2
            p2[px, 0:12, j * 128 : (j + 1) * 128] = jnp.where(
                inside & (gx >= 0) & (gx < 16), pooled[px * 12 : px * 12 + 12, :], 0.0
            )
    planes = []
    for dx in range(3):
        for dy in range(3):
            pieces = []
            for t in range(8):
                for x in range(2):
                    pieces.append(p2[x + dx, 1 + dy : 9 + dy, 128 * t : 128 * t + 256])
            planes.append(jnp.concatenate(pieces, axis=0).astype(BF16))
    r = jnp.dot(jnp.concatenate(planes, axis=1), w3_ref[...], preferred_element_type=F32)
    r3_ref[...] = r
    s1 = fold(jnp.sum(r, axis=0, keepdims=True), 64)
    s2 = fold(jnp.sum(r * r, axis=0, keepdims=True), 64)
    low = iota((8, 128), 1) < 64
    for t in range(8):
        m = jnp.maximum(r[t * 16 : t * 16 + 8, :], r[t * 16 + 8 : t * 16 + 16, :])
        a, b = m[:, 0:128], m[:, 128:256]
        a = jnp.maximum(a, pltpu.roll(a, 64, 1))
        b = jnp.maximum(b, pltpu.roll(b, 64, 1))
        yrow[:, t * 128 : (t + 1) * 128] = jnp.where(low, a, b)
    pooled = jnp.concatenate(
        [jnp.maximum(yrow[2 * i : 2 * i + 1, :], yrow[2 * i + 1 : 2 * i + 2, :]) for i in range(4)], axis=0
    )
    mean_here = s1 / 512.0
    spread = jnp.sqrt(jnp.maximum(s2 / 512.0 - mean_here * mean_here, 0.0))
    begin = mean_here + jnp.clip(-params_ref[5:6, :] / params_ref[4:5, :], -8.0, 8.0) * spread
    offset = jnp.maximum(begin, fold(jnp.sum(pooled, axis=0, keepdims=True), 64) / 64.0)
    at = iota((1, 128), 1)
    offset = offset.astype(BF16).astype(F32)
    apart = pooled - jnp.concatenate([offset] * 8, axis=1)
    wide = pltpu.roll(jnp.concatenate([apart, jnp.zeros((4, 128), F32)], axis=1), 64, 1)
    sums = jnp.where(at < 64, s1, s2)
    high = sums.astype(BF16).astype(F32)
    middle = (sums - high).astype(BF16).astype(F32)
    edge = jnp.concatenate([high, middle, sums - high - middle, offset], axis=0)
    ends = iota((4, 128), 1) < 64
    out = jnp.concatenate(
        [jnp.where(ends, edge, wide[:, 0:128]), wide[:, 128:1024], jnp.where(ends, wide[:, 1024:1152], edge)], axis=1
    ).astype(BF16)
    out_ref[...] = jnp.broadcast_to(out.reshape(1, 4, 1152), (DEVICES // 2, 4, 1152))


def third_part(half, stats, table, w3):
    return call(
        third_kernel,
        [near((128, 256), F32), far((DEVICES // 2, 4, 1152), BF16)],
        [(a, VMEM) for a in (half, stats, table, w3)],
        [((4, 16, 1152), F32), ((8, 1024), F32)],
    )


def fourth_kernel(r3_ref, own_ref, other_ref, params_ref, w4_ref, f3_ref, out_ref, p3, pd, r4):
    edge = jnp.zeros((4, 128), F32)
    tail = jnp.zeros((4, 128), F32)
    for ref in (own_ref, other_ref):
        edge = edge + jnp.sum(ref[:, :, 0:128].astype(F32), axis=0)
        tail = tail + jnp.sum(ref[:, :, 1024:1152].astype(F32), axis=0)
    total = jnp.sum(jnp.where(iota((4, 128), 1) < 64, edge, tail)[0:3, :], axis=0, keepdims=True)
    normal = normaliser(total, VOXELS_1 / 64, params_ref, 2, 2)
    f3 = settle(r3_ref[...], normal)
    for t in range(8):
        for x in range(2):
            f3_ref[x, :, t * 256 : (t + 1) * 256] = f3[t * 16 + x * 8 : t * 16 + x * 8 + 8, :].astype(BF16)
    lane = iota((4, 128), 1)
    low = iota((16, 128), 1) < 64
    y = iota((16, 128), 0)
    one = tuple(v[:, 0:128] for v in normal)
    zero = jnp.zeros((16, 4224), BF16)
    for dy in range(3):
        pd[dy, 0] = zero
        pd[dy, 9] = zero

    def place(even_ref, odd_ref):
        def step(gx, carry):
            for gy in range(4):
                ref = even_ref if gy % 2 == 0 else odd_ref
                last = jnp.zeros((4, 128), F32)
                for gz in range(4):
                    v = ref[(gx * 2 + gy // 2) * 4 + gz].astype(F32)
                    v0, v8 = v[:, 0:128], v[:, 1024:1152]
                    offset = jnp.where(lane < 64, v0, v8)[3:4, :]
                    start = gz * 1024
                    p3[4 * gy : 4 * gy + 4, start : start + 128] = jnp.where(lane < 64, last, v0 + offset)
                    p3[4 * gy : 4 * gy + 4, start + 128 : start + 1024] = v[:, 128:1024] + jnp.concatenate([offset] * 7, axis=1)
                    last = v8 + offset
                p3[4 * gy : 4 * gy + 4, 4096:4224] = last
            for j in range(33):
                lanes = slice(j * 128, (j + 1) * 128)
                v = settle(p3[:, lanes], one)
                if j == 0:
                    v = jnp.where(low, 0.0, v)
                if j == 32:
                    v = jnp.where(low, v, 0.0)
                pd[0, gx + 1, :, lanes] = jnp.where(y > 0, pltpu.roll(v, 1, 0), 0.0).astype(BF16)
                pd[1, gx + 1, :, lanes] = v.astype(BF16)
                pd[2, gx + 1, :, lanes] = jnp.where(y < 15, pltpu.roll(v, 15, 0), 0.0).astype(BF16)
            return carry

        lax.fori_loop(0, 8, step, 0)

    core = lax.axis_index("gc")

    @pl.when(core == 0)
    def _():
        place(own_ref, other_ref)

    @pl.when(core != 0)
    def _():
        place(other_ref, own_ref)

    def tiles(i, carry):
        s1, s2 = carry
        planes = []
        for dx in range(3):
            for dy in range(3):
                pieces = [
                    pd[dy, dx : dx + 8, :, pl.ds(pl.multiple_of(128 * (i * 8 + g), 128), 256)].reshape(128, 256)
                    for g in range(8)
                ]
                planes.append(jnp.concatenate(pieces, axis=0))
        r = jnp.dot(jnp.concatenate(planes, axis=1), w4_ref[...], preferred_element_type=F32)
        r4[pl.ds(pl.multiple_of(i * 1024, 1024), 1024), :] = r
        return s1 + jnp.sum(r, axis=0, keepdims=True), s2 + jnp.sum(r * r, axis=0, keepdims=True)

    zeros = jnp.zeros((1, 256), F32)
    s1, s2 = lax.fori_loop(0, 4, tiles, (zeros, zeros))
    cells = VOXELS_1 / 512
    mean = fold(s1, 128) / cells
    variance = fold(s2, 128) / cells - mean * mean
    factor = params_ref[6:7, :] * lax.rsqrt(variance + EPSILON)
    last = tuple(jnp.concatenate([v] * 2, axis=1) for v in (mean, factor, params_ref[7:8, :]))

    def finish(t, carry):
        f = settle(r4[pl.ds(pl.multiple_of(t * 128, 128), 128), :], last).astype(BF16)
        out_ref[:, :, pl.ds(pl.multiple_of(256 * t, 256), 256)] = f.reshape(8, 16, 256)
        return carry

    lax.fori_loop(0, 32, finish, 0)


def fourth_part(r3, own, other, table, w4):
    return call(
        fourth_kernel,
        [full((2, 8, 2048), BF16), full((8, 16, 8192), BF16)],
        [(a, VMEM) for a in (r3, own, other, table, w4)],
        [((16, 4224), F32), ((3, 10, 16, 4224), BF16), ((4096, 256), F32)],
    )


def neighbours(low_face, high_face, axis, count):
    up = [(i, i + 1) for i in range(count - 1)]
    down = [(i + 1, i) for i in range(count - 1)]
    return lax.ppermute(high_face, axis, up), lax.ppermute(low_face, axis, down)


def after(values, event):
    return lax.optimization_barrier((values, event))


def shards(volume, k1, g1, b1, k2, g2, b2, k3, g3, b3, k4, g4, b4):
    low, high = neighbours(volume, volume, "gz", 4)
    w1, w1_far = first_band(k1.reshape(27, 16))
    (low, high, w1) = lax.optimization_barrier((low, high, w1))
    edge = jnp.where(lax.broadcasted_iota(jnp.int32, volume.shape, 2) < 64, high, low)
    wide = jnp.concatenate([volume, edge], axis=2)
    low, high = neighbours(wide[:, 0:8, :], wide[:, 24:32, :], ("gh", "gc"), 4)
    mid = jnp.concatenate([low, wide, high], axis=1)
    (mid, k2, g1) = lax.optimization_barrier((mid, k2, g1))
    low, high = neighbours(mid, mid, "gx", 8)
    lhs_mid, far_mid, half_mid, sums = middle_part(mid, w1)
    w2 = band(k2, 1)
    table = params(g1, b1, g2, b2, g3, b3, g4, b4)
    (low, high, lhs_mid, w2, table) = lax.optimization_barrier((low, high, lhs_mid, w2, table))
    ends, half_edge, stats = first_part(low, high, lhs_mid, sums, w1)

    total1 = lax.all_to_all(stats, AXES, 0, 0, tiled=True)
    half1 = wide_first_part(low, high, ends, half_mid, half_edge, w1_far)
    half1, total1 = after(half1, total1)
    p1, r2, stats = second_part(half1, total1, table, w2)

    (p1, k3), stats = after((p1, k3), stats)
    total2 = lax.all_to_all(stats, AXES, 0, 0, tiled=True)
    half2 = wide_second_part(p1, w2)
    w3 = band(k3, 0)
    (half2, w3), total2 = after((half2, w3), total2)
    r3, packed = third_part(half2, total2, table, w3)

    (k4, far_mid, r2), packed = after((k4, far_mid, r2), packed)
    own = lax.all_to_all(packed, CHIPS, 0, 0, tiled=True)
    f1 = first_output(far_mid, ends, w1_far, total1, table)
    f2 = second_output(r2, total2, table)
    w4 = band(k4, 0)
    (f1, f2, w4), own = after((f1, f2, w4), own)
    other = lax.ppermute(own, "gc", [(0, 1), (1, 0)])
    f3, f4 = fourth_part(r3, own, other, table, w4)
    return f1, f2, f3, f4


def solution(mesh):
    parts = Mesh(mesh.devices.reshape(8, 2, 2, 4), AXES)
    spread = P("gx", ("gh", "gc"), "gz")
    return jax.shard_map(
        shards,
        mesh=parts,
        in_specs=(spread,) + (P(),) * 12,
        out_specs=(spread, spread, spread, P()),
        check_vma=False,
    )
```

```python
import functools

import jax
import jax.numpy as jnp
from jax import lax
from jax.experimental import pallas as pl
from jax.experimental.pallas import tpu as pltpu
from jax.sharding import Mesh
from jax.sharding import PartitionSpec as P

EPSILON = 1e-05
F32 = jnp.float32
BF16 = jnp.bfloat16
AXES = ("gx", "gh", "gc", "gz")
CHIPS = ("gx", "gh", "gz")
DEVICES = 128
VOXELS_1 = 64.0 * 128.0 * 512.0
PARAMS = pltpu.CompilerParams(vmem_limit_bytes=40 * 1024 * 1024)


def full(shape, dtype):
    return jax.ShapeDtypeStruct(shape, dtype)


def iota(shape, dim):
    return lax.broadcasted_iota(jnp.int32, shape, dim)


VMEM = pl.BlockSpec(memory_space=pltpu.VMEM)
ANY = pl.BlockSpec(memory_space=pl.ANY)


def near(shape, dtype):
    return pltpu.VMEM(shape, dtype)


def far(shape, dtype):
    return pltpu.HBM(shape, dtype)


def held(array):
    return pltpu.with_memory_space_constraint(array, pltpu.HBM)


def call(kernel, outs, ins, scratch=(), out_specs=None):
    return pl.pallas_call(
        kernel,
        in_specs=[spec for _, spec in ins],
        out_specs=tuple(out_specs or [VMEM] * len(outs)),
        out_shape=tuple(outs),
        scratch_shapes=[s if not isinstance(s, tuple) else pltpu.VMEM(*s) for s in scratch],
        compiler_params=PARAMS,
    )(*[array for array, _ in ins])


def position():
    gx, gh, gc, gz = (lax.axis_index(a) for a in AXES)
    return gx, gh * 2 + gc, gz


def first_band_kernel(k_ref, volume_far, w_ref, far_ref, volume_ref, sem):
    own = pltpu.make_async_copy(volume_far, volume_ref, sem)
    own.start()
    spread = (iota((16, 768), 1) % 16 == iota((16, 768), 0)).astype(BF16)
    taps = jnp.dot(k_ref[...], spread, preferred_element_type=F32)
    lag = iota((64, 768), 0) - iota((64, 768), 1) // 16
    for dx in range(3):
        for dy in range(3):
            block = jnp.zeros((64, 768), F32)
            for dz in range(3):
                t = (dx * 3 + dy) * 3 + dz
                block = jnp.where(lag == dz, taps[t : t + 1, :], block)
            w_ref[dx * 256 + dy * 64 : dx * 256 + dy * 64 + 64, :] = block.astype(BF16)
        w_ref[dx * 256 + 192 : dx * 256 + 256, :] = jnp.zeros((64, 768), BF16)
    far_ref[...] = w_ref[...]
    own.wait()


def fill_params(vectors, out_ref):
    lane = iota((1, 128), 1)
    for i, ref in enumerate(vectors):
        count = ref.shape[0]
        row = jnp.zeros((1, 128), F32)
        for c in range(count):
            row = jnp.where(lane % count == c, ref[c], row)
        out_ref[i : i + 1, :] = row


def band_kernel(cin, cout, first, k_ref, w_ref, t_ref):
    outs = 256 // cout
    tile = (iota((cout, 256), 1) % cout == iota((cout, 256), 0)).astype(BF16)
    t_ref[...] = jnp.dot(k_ref[...], tile, preferred_element_type=F32)
    zo = iota((cin, 256), 1) // cout

    def plane(p, carry):
        for zi in range(-first, 256 // cin - first):
            block = jnp.zeros((cin, 256), F32)
            if 0 <= zi < outs + 2:
                for dz in range(3):
                    start = pl.multiple_of((p * 3 + dz) * cin, cin)
                    block = jnp.where(zo == zi - dz, t_ref[pl.ds(start, cin), :], block)
            start = pl.multiple_of(p * 256 + (zi + first) * cin, cin)
            w_ref[pl.ds(start, cin), :] = block.astype(BF16)
        return carry

    lax.fori_loop(0, 9, plane, 0)


def first_band(k, volume):
    return call(
        first_band_kernel,
        [near((768, 768), BF16), far((768, 768), BF16), near(volume.shape, BF16)],
        [(k.reshape(27, 16), VMEM), (held(volume), ANY)],
        [pltpu.SemaphoreType.DMA(())],
    )


def early_kernel(*refs):
    k2_far, vectors_far = refs[0], refs[1:9]
    w2_ref, params_ref, k2_ref, t_ref = refs[9:13]
    vectors, sems = refs[13:21], refs[21]
    copies = [pltpu.make_async_copy(k2_far, k2_ref, sems.at[8])]
    copies += [pltpu.make_async_copy(v, p, sems.at[i]) for i, (v, p) in enumerate(zip(vectors_far, vectors))]
    for c in copies:
        c.start()
    for c in copies:
        c.wait()
    band_kernel(16, 32, 1, k2_ref, w2_ref, t_ref)
    fill_params(vectors, params_ref)


def early_part(k2, vectors):
    return call(
        early_kernel,
        [near((2304, 256), BF16), near((8, 128), F32)],
        [(held(k2.reshape(432, 32)), ANY)] + [(held(v), ANY) for v in vectors],
        [((432, 32), BF16), ((432, 256), F32)]
        + [pltpu.SMEM(v.shape, F32) for v in vectors]
        + [pltpu.SemaphoreType.DMA((9,))],
    )


def band(k, first):
    cin, cout = k.shape[3:]
    return call(
        functools.partial(band_kernel, cin, cout, first),
        [near((2304, 256), BF16)],
        [(held(k.reshape(27 * cin, cout)), VMEM)],
        [((27 * cin, 256), F32)],
    )[0]


def fold(row, width):
    total = row[:, 0:128]
    for j in range(1, row.shape[1] // 128):
        total = total + row[:, j * 128 : (j + 1) * 128]
    step = 64
    while step >= width:
        total = total + pltpu.roll(total, step, 1)
        step //= 2
    return total


def pack_stats(s1, s2, width):
    return jnp.where(iota((1, 128), 1) < 64, fold(s1, width), fold(s2, width))


def normaliser(total, cells, params_ref, level, copies):
    lane = iota((1, 128), 1)
    other = pltpu.roll(total, 64, 1)
    mean = jnp.where(lane < 64, total, other) / cells
    variance = jnp.where(lane < 64, other, total) / cells - mean * mean
    shift = params_ref[2 * level + 1 : 2 * level + 2, :]
    factor = params_ref[2 * level : 2 * level + 1, :] * lax.rsqrt(variance + EPSILON)
    return tuple(jnp.concatenate([v] * copies, axis=1) for v in (mean, factor, shift))


def settle(response, normal):
    mean, factor, shift = normal
    return jnp.maximum((response - mean) * factor + shift, 0.0)


def slots(stats):
    return jnp.broadcast_to(stats.reshape(1, 1, 128), (DEVICES, 1, 128))


def paired_rows(ref, j, count):
    return jnp.maximum(ref[j, pl.ds(0, count, stride=2), :], ref[j, pl.ds(1, count, stride=2), :])


def fill(out_ref, at, v):
    lane = iota((48, 128), 1)
    for q, part, turn in ((0, v, 9), (1, v[:, 0:128], 128 - 39), (2, v, 256 - 87)):
        wa = pltpu.roll(part, turn, 1)[:, 0:128]
        wb = pltpu.roll(wa, 64, 1)
        out_ref[q, at, :, 0:128] = jnp.where(lane < 64, pltpu.roll(wa, 1, 0), wb).astype(BF16)
        out_ref[q, at, :, 128:256] = pltpu.roll(wa, 47, 0).astype(BF16)


def response_1(planes, w1_ref):
    lhs = jnp.concatenate(planes, axis=2)
    n, rows, _ = lhs.shape
    r = jnp.dot(lhs.reshape(n * rows, 768), w1_ref[...], preferred_element_type=F32)
    return r.reshape(n, rows, 768)


def sums_1(own, q):
    own = own.reshape(-1, 768)
    row1 = jnp.sum(own, axis=0, keepdims=True)
    row2 = jnp.sum(own * own, axis=0, keepdims=True)
    at = iota((1, 768), 1)
    if q == 0:
        row1, row2 = (jnp.where(at >= 128, r_, 0.0) for r_ in (row1, row2))
    if q == 2:
        row1, row2 = (jnp.where(at < 640, r_, 0.0) for r_ in (row1, row2))
    return row1, row2


def halve_rows(r, rows, half_ref, q):
    n = r.shape[0]
    flat = r.reshape(n * 48, 768)
    for j in range(6):
        rows[j, 0 : n * 48] = flat[:, j * 128 : (j + 1) * 128]
    for j in range(6):
        half_ref[q * 6 + j] = paired_rows(rows, j, n * 24)


def widen_kernel(volume_ref, inner_ref, outer_ref, wide_ref, outer_face_ref):
    odd = lax.axis_index("gz") % 2
    volume, inner, outer = (ref[...].astype(F32) for ref in (volume_ref, inner_ref, outer_ref))
    edge = jnp.where((iota((8, 32, 128), 2) < 64) == (odd == 0), inner, outer)
    wide = jnp.concatenate([volume, edge], axis=2)
    wide_ref[...] = wide.astype(BF16)
    core = lax.axis_index("gc")
    outer_face_ref[...] = jnp.where(core == 0, wide[:, 0:8], wide[:, 24:32]).astype(BF16)


def widen(volume, inner, outer):
    return call(
        widen_kernel,
        [near((8, 32, 256), BF16), near((8, 8, 256), BF16)],
        [(volume, VMEM), (inner, VMEM), (outer, VMEM)],
    )


def inner_face_kernel(wide_ref, face_ref):
    wide = wide_ref[...].astype(F32)
    face_ref[...] = jnp.where(lax.axis_index("gc") == 0, wide[:, 24:32], wide[:, 0:8]).astype(BF16)


def inner_face(wide):
    return call(inner_face_kernel, [near((8, 8, 256), BF16)], [(wide, VMEM)])[0]


def assemble_kernel(wide_ref, inner_ref, outer_ref, mid_ref, packed_ref):
    core = lax.axis_index("gc")
    inner, outer = inner_ref[...].astype(F32), outer_ref[...].astype(F32)
    low = jnp.where(core == 0, outer, inner)
    high = jnp.where(core == 0, inner, outer)
    mid = jnp.concatenate([low, wide_ref[...].astype(F32), high], axis=1)
    mid_ref[...] = mid.astype(BF16)
    packed_ref[0:8] = mid[:, :, 0:128].astype(BF16)
    slot = (iota((48, 128), 1) + 8) % 128 // 16
    ends = mid[0, :, 128:256]
    for i in range(1, 8):
        ends = jnp.where(slot == i, pltpu.roll(mid[i, :, 128:256], 16 * i, 1), ends)
    packed_ref[8] = ends.astype(BF16)


def assemble(wide, inner, outer):
    return call(
        assemble_kernel,
        [near((8, 48, 256), BF16), near((9, 48, 128), BF16)],
        [(wide, VMEM), (inner, VMEM), (outer, VMEM)],
    )


def plane(own, ends, i):
    ends = ends.astype(F32)
    if i:
        ends = pltpu.roll(ends, 128 - 16 * i, 1)
    return jnp.concatenate([own.astype(F32), ends], axis=1)


def middle_kernel(mid_ref, w1_ref, lhs_ref, far_ref, sums_ref):
    for i in range(8):
        fill(lhs_ref, i, mid_ref[i].astype(F32))
    far_ref[...] = lhs_ref[...]
    s1 = jnp.zeros((1, 768), F32)
    s2 = jnp.zeros((1, 768), F32)
    for q in range(3):
        r = response_1([lhs_ref[q, dx : 6 + dx][:, 8:40] for dx in range(3)], w1_ref)
        row1, row2 = sums_1(r, q)
        s1, s2 = s1 + row1, s2 + row2
    sums_ref[0:1, :] = s1
    sums_ref[1:2, :] = s2


def middle_part(mid, w1):
    return call(
        middle_kernel,
        [near((3, 8, 48, 256), BF16), far((3, 8, 48, 256), BF16), near((8, 768), F32)],
        [(mid, VMEM), (w1, VMEM)],
    )


def first_kernel(inner_ref, outer_ref, mid_ref, sums_ref, w1_ref, ends_ref, sides_ref, stats_ref):
    even = lax.axis_index("gx") % 2 == 0

    @pl.when(even)
    def _():
        sides_ref[0] = outer_ref[...]
        sides_ref[1] = inner_ref[...]

    @pl.when(jnp.logical_not(even))
    def _():
        sides_ref[0] = inner_ref[...]
        sides_ref[1] = outer_ref[...]

    fill(ends_ref, 0, plane(sides_ref[0, 7], sides_ref[0, 8], 7))
    fill(ends_ref, 1, plane(sides_ref[1, 0], sides_ref[1, 8], 0))
    planes = []
    for q in range(3):
        a = [ends_ref[q, 0:1], mid_ref[q, 0:1], mid_ref[q, 1:2]]
        b = [mid_ref[q, 6:7], mid_ref[q, 7:8], ends_ref[q, 1:2]]
        planes.append([jnp.concatenate([a[dx], b[dx]], axis=0)[:, 8:40] for dx in range(3)])
    r = response_1([jnp.concatenate([planes[q][dx] for q in range(3)], axis=0) for dx in range(3)], w1_ref)
    s1 = sums_ref[0:1, :]
    s2 = sums_ref[1:2, :]
    for q in range(3):
        row1, row2 = sums_1(r[2 * q : 2 * q + 2], q)
        s1, s2 = s1 + row1, s2 + row2
    stats_ref[...] = slots(pack_stats(s1, s2, 16))


def first_part(inner, outer, lhs_mid, sums, w1):
    return call(
        first_kernel,
        [far((3, 2, 48, 256), BF16), far((2, 9, 48, 128), BF16), far((DEVICES, 1, 128), F32)],
        [(inner, VMEM), (outer, VMEM), (lhs_mid, VMEM), (sums, VMEM), (w1, VMEM)],
    )


def wide_first_kernel(sides_ref, mid_far, ends_far, w1_far, half_ref, lhs, rows, w1_ref, sems):
    copies = [pltpu.make_async_copy(w1_far, w1_ref, sems.at[0])]
    for q in range(3):
        copies.append(pltpu.make_async_copy(mid_far.at[q], lhs.at[q, 7:15], sems.at[3 * q + 1]))
        copies.append(pltpu.make_async_copy(ends_far.at[q, 0], lhs.at[q, 6], sems.at[3 * q + 2]))
        copies.append(pltpu.make_async_copy(ends_far.at[q, 1], lhs.at[q, 15], sems.at[3 * q + 3]))
    for c in copies:
        c.start()
    for i in range(6):
        fill(lhs, i, plane(sides_ref[0, 1 + i], sides_ref[0, 8], 1 + i))
        fill(lhs, 16 + i, plane(sides_ref[1, 1 + i], sides_ref[1, 8], 1 + i))
    for c in copies:
        c.wait()
    for q in range(3):
        r = response_1([lhs[q, dx : 20 + dx] for dx in range(3)], w1_ref)
        r = jnp.max(r.reshape(10, 2, 48, 768), axis=1).reshape(480, 768)
        for j in range(6):
            rows[j] = r[:, j * 128 : (j + 1) * 128]
        for j in range(6):
            half_ref[q * 6 + j] = paired_rows(rows, j, 240)


def wide_first_part(sides, lhs_mid, ends, w1):
    return call(
        wide_first_kernel,
        [near((18, 240, 128), F32)],
        [(held(sides), VMEM)] + [(held(a), ANY) for a in (lhs_mid, ends, w1)],
        [((3, 22, 48, 256), BF16), ((6, 480, 128), F32), ((768, 768), BF16), pltpu.SemaphoreType.DMA((10,))],
    )[0]


def first_output_kernel(mid_ref, ends_ref, w1_ref, stats_ref, params_ref, f1_ref):
    normal = normaliser(jnp.sum(stats_ref[...], axis=0), VOXELS_1, params_ref, 0, 6)
    for q in range(3):
        middle = mid_ref[q]
        planes = [
            jnp.concatenate([ends_ref[q, 0:1], middle[0:7]], axis=0),
            middle,
            jnp.concatenate([middle[1:8], ends_ref[q, 1:2]], axis=0),
        ]
        f = settle(response_1([p[:, 8:40, :] for p in planes], w1_ref), normal)
        a, b = (128 if q == 0 else 0), (640 if q == 2 else 768)
        f1_ref[:, :, q * 768 - 128 + a : q * 768 - 128 + b] = f[:, :, a:b].astype(BF16)


def first_output(lhs_mid, ends, w1, stats, table):
    return call(
        first_output_kernel,
        [full((8, 32, 2048), BF16)],
        [(held(a), VMEM) for a in (lhs_mid, ends, w1)] + [(stats, VMEM), (table, VMEM)],
    )[0]


def selector(chans):
    row, col = iota((256, 256), 0), iota((256, 256), 1)
    return (row == (col % 128) // chans * (2 * chans) + col % chans + col // 128 * chans).astype(BF16)


def halved(left, right, normal, pick):
    features = jnp.concatenate([settle(left, normal), settle(right, normal)], axis=1).astype(BF16)
    both = jnp.dot(features, pick, preferred_element_type=F32)
    return jnp.maximum(both[:, 0:128], both[:, 128:256])


def second_kernel(half_ref, stats_ref, params_ref, w2_ref, p1_far, out_stats_ref, p1, p1_ref, pd, sem):
    normal = normaliser(jnp.sum(stats_ref[...], axis=0), VOXELS_1, params_ref, 0, 1)
    pick = selector(16)
    bx, by, bz = position()
    p1[:, :, 1152:1280] = jnp.zeros((10, 24, 128), F32)
    gy = iota((10, 24, 128), 1) - 4 + by * 16
    gx = iota((10, 24, 128), 0) - 3 + bx * 4
    inside = (gy >= 0) & (gy < 64) & (gx >= 0) & (gx < 32)
    for j in range(9):
        pooled = halved(half_ref[2 * j], half_ref[2 * j + 1], normal, pick).reshape(10, 24, 128)
        gz = iota((10, 24, 128), 2) // 16 - 4 + 8 * j + bz * 64
        p1[:, :, j * 128 : (j + 1) * 128] = jnp.where(inside & (gz >= 0) & (gz < 256), pooled, 0.0)
    for dy in range(3):
        pd[dy] = p1[2:8, 3 + dy : 19 + dy, :].astype(BF16)
    p1_ref[...] = p1[...].astype(BF16)
    save = pltpu.make_async_copy(p1_ref, p1_far, sem)
    save.start()
    planes = []
    for dx in range(3):
        for dy in range(3):
            pieces = [pd[dy, dx : dx + 4, :, 128 * t : 128 * t + 256].reshape(64, 256) for t in range(9)]
            planes.append(jnp.concatenate(pieces, axis=0))
    r = jnp.dot(jnp.concatenate(planes, axis=1), w2_ref[...], preferred_element_type=F32)
    s1 = jnp.zeros((1, 256), F32)
    s2 = jnp.zeros((1, 256), F32)
    lane = iota((1, 256), 1)
    for t in range(9):
        own = r[64 * t : 64 * t + 64]
        row1 = jnp.sum(own, axis=0, keepdims=True)
        row2 = jnp.sum(own * own, axis=0, keepdims=True)
        if t == 0:
            row1, row2 = (jnp.where(lane >= 64, r_, 0.0) for r_ in (row1, row2))
        if t == 8:
            row1, row2 = (jnp.where(lane < 64, r_, 0.0) for r_ in (row1, row2))
        s1, s2 = s1 + row1, s2 + row2
    out_stats_ref[...] = slots(pack_stats(s1, s2, 32))
    save.wait()


def second_part(half, stats, table, w2):
    return call(
        second_kernel,
        [far((10, 24, 1280), BF16), far((DEVICES, 1, 128), F32)],
        [(a, VMEM) for a in (half, stats, table, w2)],
        [((10, 24, 1280), F32), ((10, 24, 1280), BF16), ((3, 6, 16, 1280), BF16), pltpu.SemaphoreType.DMA(())],
        [ANY, VMEM],
    )


def wide_second_kernel(p1_ref, w2_ref, k3_far, half_ref, r2_ref, w3_ref, pd, rows, k3_ref, t_ref, sem):
    kernel = pltpu.make_async_copy(k3_far, k3_ref, sem)
    kernel.start()

    def shift(i, carry):
        v = p1_ref[i].astype(F32)
        pd[0, i] = pltpu.roll(v, 1, 0)
        pd[1, i] = v
        pd[2, i] = pltpu.roll(v, 23, 0)
        return carry

    lax.fori_loop(0, 10, shift, 0)
    for t in range(0, 9, 3):
        planes = []
        for dx in range(3):
            for dy in range(3):
                pieces = [pd[dy, dx : dx + 8, :, 128 * u : 128 * u + 256].reshape(192, 256) for u in range(t, t + 3)]
                planes.append(jnp.concatenate(pieces, axis=0).astype(BF16))
        r = jnp.dot(jnp.concatenate(planes, axis=1), w2_ref[...], preferred_element_type=F32)
        own = r.reshape(3, 8, 24, 256)[:, 2:6, 4:20]
        r2_ref[64 * t : 64 * t + 192, :] = own.reshape(192, 256)
        r = jnp.max(r.reshape(3, 4, 2, 24, 256), axis=2).reshape(3, 96, 256)
        for i in range(3):
            for j in range(2):
                rows[2 * i + j] = r[i, :, j * 128 : (j + 1) * 128]
        for j in range(6):
            half_ref[2 * t + j] = paired_rows(rows, j, 48)
    kernel.wait()
    band_kernel(32, 64, 0, k3_ref, w3_ref, t_ref)


def wide_second_part(p1, w2, k3):
    return call(
        wide_second_kernel,
        [near((18, 48, 128), F32), far((576, 256), F32), near((2304, 256), BF16)],
        [(held(p1), VMEM), (w2, VMEM), (held(k3.reshape(864, 64)), ANY)],
        [((3, 10, 24, 1280), F32), ((6, 96, 128), F32), ((864, 64), BF16), ((864, 256), F32)]
        + [pltpu.SemaphoreType.DMA(())],
    )


def second_output_kernel(r2_ref, stats_ref, params_ref, f2_ref):
    normal = normaliser(jnp.sum(stats_ref[...], axis=0), VOXELS_1 / 8, params_ref, 1, 2)
    f = [settle(r2_ref[64 * t : 64 * t + 64, :], normal) for t in range(9)]
    wide = pltpu.roll(jnp.concatenate(f, axis=1), 2304 - 64, 1)[:, 0:2048]
    f2_ref[...] = wide.reshape(4, 16, 2048).astype(BF16)


def second_output(r2, stats, table):
    return call(
        second_output_kernel,
        [full((4, 16, 2048), BF16)],
        [(held(r2), VMEM), (stats, VMEM), (table, VMEM)],
    )[0]


def third_kernel(half_ref, stats_ref, params_ref, w3_ref, r3_ref, out_ref, p2, yrow):
    normal = normaliser(jnp.sum(stats_ref[...], axis=0), VOXELS_1 / 8, params_ref, 1, 1)
    bx, by, bz = position()
    pick = selector(32)
    gy = iota((12, 128), 0) - 2 + by * 8
    for j in range(9):
        pooled = halved(half_ref[2 * j], half_ref[2 * j + 1], normal, pick)
        gz = iota((12, 128), 1) // 32 + 4 * j - 1 + bz * 32
        inside = (gy >= 0) & (gy < 32) & (gz >= 0) & (gz < 128)
        for px in range(4):
            gx = px - 1 + bx * 2
            p2[px, 0:12, j * 128 : (j + 1) * 128] = jnp.where(
                inside & (gx >= 0) & (gx < 16), pooled[px * 12 : px * 12 + 12, :], 0.0
            )
    planes = []
    for dx in range(3):
        for dy in range(3):
            pieces = []
            for t in range(8):
                for x in range(2):
                    pieces.append(p2[x + dx, 1 + dy : 9 + dy, 128 * t : 128 * t + 256])
            planes.append(jnp.concatenate(pieces, axis=0).astype(BF16))
    r = jnp.dot(jnp.concatenate(planes, axis=1), w3_ref[...], preferred_element_type=F32)
    r3_ref[...] = r
    s1 = fold(jnp.sum(r, axis=0, keepdims=True), 64)
    s2 = fold(jnp.sum(r * r, axis=0, keepdims=True), 64)
    low = iota((8, 128), 1) < 64
    for t in range(8):
        m = jnp.maximum(r[t * 16 : t * 16 + 8, :], r[t * 16 + 8 : t * 16 + 16, :])
        a, b = m[:, 0:128], m[:, 128:256]
        a = jnp.maximum(a, pltpu.roll(a, 64, 1))
        b = jnp.maximum(b, pltpu.roll(b, 64, 1))
        yrow[:, t * 128 : (t + 1) * 128] = jnp.where(low, a, b)
    pooled = jnp.concatenate(
        [jnp.maximum(yrow[2 * i : 2 * i + 1, :], yrow[2 * i + 1 : 2 * i + 2, :]) for i in range(4)], axis=0
    )
    mean_here = s1 / 512.0
    spread = jnp.sqrt(jnp.maximum(s2 / 512.0 - mean_here * mean_here, 0.0))
    begin = mean_here + jnp.clip(-params_ref[5:6, :] / params_ref[4:5, :], -8.0, 8.0) * spread
    offset = jnp.maximum(begin, fold(jnp.sum(pooled, axis=0, keepdims=True), 64) / 64.0)
    at = iota((1, 128), 1)
    offset = offset.astype(BF16).astype(F32)
    apart = pooled - jnp.concatenate([offset] * 8, axis=1)
    wide = pltpu.roll(jnp.concatenate([apart, jnp.zeros((4, 128), F32)], axis=1), 64, 1)
    sums = jnp.where(at < 64, s1, s2)
    high = sums.astype(BF16).astype(F32)
    middle = (sums - high).astype(BF16).astype(F32)
    edge = jnp.concatenate([high, middle, sums - high - middle, offset], axis=0)
    ends = iota((4, 128), 1) < 64
    out = jnp.concatenate(
        [jnp.where(ends, edge, wide[:, 0:128]), wide[:, 128:1024], jnp.where(ends, wide[:, 1024:1152], edge)], axis=1
    ).astype(BF16)
    out_ref[...] = jnp.broadcast_to(out.reshape(1, 4, 1152), (DEVICES // 2, 4, 1152))


def third_part(half, stats, table, w3):
    return call(
        third_kernel,
        [near((128, 256), F32), far((DEVICES // 2, 4, 1152), BF16)],
        [(a, VMEM) for a in (half, stats, table, w3)],
        [((4, 16, 1152), F32), ((8, 1024), F32)],
    )


def fourth_kernel(r3_ref, own_ref, other_ref, params_ref, w4_ref, f3_ref, out_far, p3, pd, r4, out_ref, sems):
    edge = jnp.zeros((4, 128), F32)
    tail = jnp.zeros((4, 128), F32)
    for ref in (own_ref, other_ref):
        edge = edge + jnp.sum(ref[:, :, 0:128].astype(F32), axis=0)
        tail = tail + jnp.sum(ref[:, :, 1024:1152].astype(F32), axis=0)
    total = jnp.sum(jnp.where(iota((4, 128), 1) < 64, edge, tail)[0:3, :], axis=0, keepdims=True)
    normal = normaliser(total, VOXELS_1 / 64, params_ref, 2, 2)
    f3 = settle(r3_ref[...], normal)
    for t in range(8):
        for x in range(2):
            f3_ref[x, :, t * 256 : (t + 1) * 256] = f3[t * 16 + x * 8 : t * 16 + x * 8 + 8, :].astype(BF16)
    lane = iota((4, 128), 1)
    low = iota((16, 128), 1) < 64
    y = iota((16, 128), 0)
    one = tuple(v[:, 0:128] for v in normal)
    zero = jnp.zeros((16, 4224), BF16)
    for dy in range(3):
        pd[dy, 0] = zero
        pd[dy, 9] = zero

    def place(even_ref, odd_ref):
        def step(gx, carry):
            for gy in range(4):
                ref = even_ref if gy % 2 == 0 else odd_ref
                last = jnp.zeros((4, 128), F32)
                for gz in range(4):
                    v = ref[(gx * 2 + gy // 2) * 4 + gz].astype(F32)
                    v0, v8 = v[:, 0:128], v[:, 1024:1152]
                    offset = jnp.where(lane < 64, v0, v8)[3:4, :]
                    start = gz * 1024
                    p3[4 * gy : 4 * gy + 4, start : start + 128] = jnp.where(lane < 64, last, v0 + offset)
                    p3[4 * gy : 4 * gy + 4, start + 128 : start + 1024] = v[:, 128:1024] + jnp.concatenate([offset] * 7, axis=1)
                    last = v8 + offset
                p3[4 * gy : 4 * gy + 4, 4096:4224] = last
            for j in range(33):
                lanes = slice(j * 128, (j + 1) * 128)
                v = settle(p3[:, lanes], one)
                if j == 0:
                    v = jnp.where(low, 0.0, v)
                if j == 32:
                    v = jnp.where(low, v, 0.0)
                pd[0, gx + 1, :, lanes] = jnp.where(y > 0, pltpu.roll(v, 1, 0), 0.0).astype(BF16)
                pd[1, gx + 1, :, lanes] = v.astype(BF16)
                pd[2, gx + 1, :, lanes] = jnp.where(y < 15, pltpu.roll(v, 15, 0), 0.0).astype(BF16)
            return carry

        lax.fori_loop(0, 8, step, 0)

    core = lax.axis_index("gc")

    @pl.when(core == 0)
    def _():
        place(own_ref, other_ref)

    @pl.when(core != 0)
    def _():
        place(other_ref, own_ref)

    s1 = jnp.zeros((1, 256), F32)
    s2 = jnp.zeros((1, 256), F32)
    for i in range(0, 32, 8):
        planes = []
        for dx in range(3):
            for dy in range(3):
                pieces = [
                    pd[dy, dx : dx + 8, :, 128 * t : 128 * t + 256].reshape(128, 256) for t in range(i, i + 8)
                ]
                planes.append(jnp.concatenate(pieces, axis=0))
        r = jnp.dot(jnp.concatenate(planes, axis=1), w4_ref[...], preferred_element_type=F32)
        r4[i * 128 : i * 128 + 1024, :] = r
        s1, s2 = s1 + jnp.sum(r, axis=0, keepdims=True), s2 + jnp.sum(r * r, axis=0, keepdims=True)
    cells = VOXELS_1 / 512
    mean = fold(s1, 128) / cells
    variance = fold(s2, 128) / cells - mean * mean
    factor = params_ref[6:7, :] * lax.rsqrt(variance + EPSILON)
    last = tuple(jnp.concatenate([v] * 2, axis=1) for v in (mean, factor, params_ref[7:8, :]))

    copies = []
    for i in range(4):
        for t in range(8 * i, 8 * i + 8):
            f = settle(r4[t * 128 : t * 128 + 128, :], last).astype(BF16)
            out_ref[:, :, 256 * t : 256 * t + 256] = f.reshape(8, 16, 256)
        lanes = pl.ds(2048 * i, 2048)
        copies.append(pltpu.make_async_copy(out_ref.at[:, :, lanes], out_far.at[:, :, lanes], sems.at[i]))
        copies[i].start()
    for c in copies:
        c.wait()


def fourth_part(r3, own, other, table, w4):
    return call(
        fourth_kernel,
        [full((2, 8, 2048), BF16), far((8, 16, 8192), BF16)],
        [(a, VMEM) for a in (r3, own, other, table, w4)],
        [((16, 4224), F32), ((3, 10, 16, 4224), BF16), ((4096, 256), F32), ((8, 16, 8192), BF16)]
        + [pltpu.SemaphoreType.DMA((4,))],
        [VMEM, ANY],
    )


def across(block, axis, swaps):
    return lax.ppermute(block, axis, swaps + [(b, a) for a, b in swaps])


def after(values, event):
    return lax.optimization_barrier((values, event))


def shards(volume, k1, g1, b1, k2, g2, b2, k3, g3, b3, k4, g4, b4):
    outer = across(volume, "gz", [(1, 2)])
    inner = across(volume, "gz", [(0, 1), (2, 3)])
    w1, w1_far, block = first_band(k1, volume)
    (inner, outer, w1) = lax.optimization_barrier((inner, outer, w1))
    wide, outer = widen(block, inner, outer)
    outer = across(outer, ("gh", "gc"), [(1, 2)])
    inner = across(inner_face(wide), "gc", [(0, 1)])
    mid, packed = assemble(wide, inner, outer)
    (packed, k2) = lax.optimization_barrier((packed, k2))
    inner = across(packed, "gx", [(0, 1), (2, 3), (4, 5), (6, 7)])
    outer = across(packed, "gx", [(1, 2), (3, 4), (5, 6)])
    w2, table = early_part(k2, (g1, b1, g2, b2, g3, b3, g4, b4))
    lhs_mid, far_mid, sums = middle_part(mid, w1)
    (inner, outer, lhs_mid, w2) = lax.optimization_barrier((inner, outer, lhs_mid, w2))
    ends, sides, stats = first_part(inner, outer, lhs_mid, sums, w1)

    total1 = lax.all_to_all(stats, AXES, 0, 0, tiled=True)
    half1 = wide_first_part(sides, far_mid, ends, w1_far)
    half1, total1 = after(half1, total1)
    p1, stats = second_part(half1, total1, table, w2)

    p1, stats = after(p1, stats)
    total2 = lax.all_to_all(stats, AXES, 0, 0, tiled=True)
    half2, r2, w3 = wide_second_part(p1, w2, k3)
    (half2, w3), total2 = after((half2, w3), total2)
    r3, packed = third_part(half2, total2, table, w3)

    (k4, far_mid, r2), packed = after((k4, far_mid, r2), packed)
    own = lax.all_to_all(packed, CHIPS, 0, 0, tiled=True)
    f1 = first_output(far_mid, ends, w1_far, total1, table)
    f2 = second_output(r2, total2, table)
    w4 = band(k4, 0)
    (f1, f2, w4), own = after((f1, f2, w4), own)
    other = lax.ppermute(own, "gc", [(0, 1), (1, 0)])
    f3, f4 = fourth_part(r3, own, other, table, w4)
    return f1, f2, f3, f4


def solution(mesh):
    parts = Mesh(mesh.devices.reshape(8, 2, 2, 4), AXES)
    spread = P("gx", ("gh", "gc"), "gz")
    return jax.shard_map(
        shards,
        mesh=parts,
        in_specs=(spread,) + (P(),) * 12,
        out_specs=(spread, spread, spread, P()),
        check_vma=False,
    )
```

```python
import functools

import jax
import jax.numpy as jnp
from jax import lax
from jax.experimental import pallas as pl
from jax.experimental.pallas import tpu as pltpu
from jax.sharding import Mesh
from jax.sharding import PartitionSpec as P

EPSILON = 1e-05
F32 = jnp.float32
BF16 = jnp.bfloat16
AXES = ("gx", "gh", "gc", "gz")
CHIPS = ("gx", "gh", "gz")
DEVICES = 128
VOXELS_1 = 64.0 * 128.0 * 512.0
PARAMS = pltpu.CompilerParams(vmem_limit_bytes=40 * 1024 * 1024)


def full(shape, dtype):
    return jax.ShapeDtypeStruct(shape, dtype)


def iota(shape, dim):
    return lax.broadcasted_iota(jnp.int32, shape, dim)


VMEM = pl.BlockSpec(memory_space=pltpu.VMEM)
ANY = pl.BlockSpec(memory_space=pl.ANY)


def near(shape, dtype):
    return pltpu.VMEM(shape, dtype)


def far(shape, dtype):
    return pltpu.HBM(shape, dtype)


def held(array):
    return pltpu.with_memory_space_constraint(array, pltpu.HBM)


def call(kernel, outs, ins, scratch=(), out_specs=None, cost=None):
    return pl.pallas_call(
        kernel,
        in_specs=[spec for _, spec in ins],
        out_specs=tuple(out_specs or [VMEM] * len(outs)),
        out_shape=tuple(outs),
        scratch_shapes=[s if not isinstance(s, tuple) else pltpu.VMEM(*s) for s in scratch],
        compiler_params=PARAMS,
        cost_estimate=cost,
    )(*[array for array, _ in ins])


def position():
    gx, gh, gc, gz = (lax.axis_index(a) for a in AXES)
    return gx, gh * 2 + gc, gz


def first_band_kernel(k_ref, volume_far, w_ref, far_ref, volume_ref, sem):
    own = pltpu.make_async_copy(volume_far, volume_ref, sem)
    own.start()
    spread = (iota((16, 768), 1) % 16 == iota((16, 768), 0)).astype(BF16)
    taps = jnp.dot(k_ref[...], spread, preferred_element_type=F32)
    lag = iota((64, 768), 0) - iota((64, 768), 1) // 16
    for dx in range(3):
        for dy in range(3):
            block = jnp.zeros((64, 768), F32)
            for dz in range(3):
                t = (dx * 3 + dy) * 3 + dz
                block = jnp.where(lag == dz, taps[t : t + 1, :], block)
            w_ref[dx * 256 + dy * 64 : dx * 256 + dy * 64 + 64, :] = block.astype(BF16)
        w_ref[dx * 256 + 192 : dx * 256 + 256, :] = jnp.zeros((64, 768), BF16)
    far_ref[...] = w_ref[...]
    own.wait()


def fill_params(vectors, out_ref):
    lane = iota((1, 128), 1)
    for i, ref in enumerate(vectors):
        count = ref.shape[0]
        row = jnp.zeros((1, 128), F32)
        for c in range(count):
            row = jnp.where(lane % count == c, ref[c], row)
        out_ref[i : i + 1, :] = row


def band_kernel(cin, cout, first, k_ref, w_ref, t_ref):
    outs = 256 // cout
    tile = (iota((cout, 256), 1) % cout == iota((cout, 256), 0)).astype(BF16)
    t_ref[...] = jnp.dot(k_ref[...], tile, preferred_element_type=F32)
    zo = iota((cin, 256), 1) // cout

    def plane(p, carry):
        for zi in range(-first, 256 // cin - first):
            block = jnp.zeros((cin, 256), F32)
            if 0 <= zi < outs + 2:
                for dz in range(3):
                    start = pl.multiple_of((p * 3 + dz) * cin, cin)
                    block = jnp.where(zo == zi - dz, t_ref[pl.ds(start, cin), :], block)
            start = pl.multiple_of(p * 256 + (zi + first) * cin, cin)
            w_ref[pl.ds(start, cin), :] = block.astype(BF16)
        return carry

    lax.fori_loop(0, 9, plane, 0)


def first_band(k, volume):
    return call(
        first_band_kernel,
        [near((768, 768), BF16), far((768, 768), BF16), near(volume.shape, BF16)],
        [(k.reshape(27, 16), VMEM), (held(volume), ANY)],
        [pltpu.SemaphoreType.DMA(())],
    )


def early_kernel(*refs):
    k2_far, vectors_far = refs[0], refs[1:9]
    w2_ref, params_ref, k2_ref, t_ref = refs[9:13]
    vectors, sems = refs[13:21], refs[21]
    copies = [pltpu.make_async_copy(k2_far, k2_ref, sems.at[8])]
    copies += [pltpu.make_async_copy(v, p, sems.at[i]) for i, (v, p) in enumerate(zip(vectors_far, vectors))]
    for c in copies:
        c.start()
    for c in copies:
        c.wait()
    band_kernel(16, 32, 1, k2_ref, w2_ref, t_ref)
    fill_params(vectors, params_ref)


def early_part(k2, vectors):
    return call(
        early_kernel,
        [near((2304, 256), BF16), near((8, 128), F32)],
        [(held(k2.reshape(432, 32)), ANY)] + [(held(v), ANY) for v in vectors],
        [((432, 32), BF16), ((432, 256), F32)]
        + [pltpu.SMEM(v.shape, F32) for v in vectors]
        + [pltpu.SemaphoreType.DMA((9,))],
    )


def band(k, first):
    cin, cout = k.shape[3:]
    return call(
        functools.partial(band_kernel, cin, cout, first),
        [near((2304, 256), BF16)],
        [(held(k.reshape(27 * cin, cout)), VMEM)],
        [((27 * cin, 256), F32)],
    )[0]


def fold(row, width):
    total = row[:, 0:128]
    for j in range(1, row.shape[1] // 128):
        total = total + row[:, j * 128 : (j + 1) * 128]
    step = 64
    while step >= width:
        total = total + pltpu.roll(total, step, 1)
        step //= 2
    return total


def pack_stats(s1, s2, width):
    return jnp.where(iota((1, 128), 1) < 64, fold(s1, width), fold(s2, width))


def normaliser(total, cells, params_ref, level, copies):
    lane = iota((1, 128), 1)
    other = pltpu.roll(total, 64, 1)
    mean = jnp.where(lane < 64, total, other) / cells
    variance = jnp.where(lane < 64, other, total) / cells - mean * mean
    shift = params_ref[2 * level + 1 : 2 * level + 2, :]
    factor = params_ref[2 * level : 2 * level + 1, :] * lax.rsqrt(variance + EPSILON)
    return tuple(jnp.concatenate([v] * copies, axis=1) for v in (mean, factor, shift))


def settle(response, normal):
    mean, factor, shift = normal
    return jnp.maximum((response - mean) * factor + shift, 0.0)


def slots(stats):
    return jnp.broadcast_to(stats.reshape(1, 1, 128), (DEVICES, 1, 128))


def paired_rows(ref, j, count):
    return jnp.maximum(ref[j, pl.ds(0, count, stride=2), :], ref[j, pl.ds(1, count, stride=2), :])


def fill(out_ref, at, v):
    lane = iota((48, 128), 1)
    for q, part, turn in ((0, v, 9), (1, v[:, 0:128], 128 - 39), (2, v, 256 - 87)):
        wa = pltpu.roll(part, turn, 1)[:, 0:128]
        wb = pltpu.roll(wa, 64, 1)
        out_ref[q, at, :, 0:128] = jnp.where(lane < 64, pltpu.roll(wa, 1, 0), wb).astype(BF16)
        out_ref[q, at, :, 128:256] = pltpu.roll(wa, 47, 0).astype(BF16)


def response_1(planes, w1_ref):
    lhs = jnp.concatenate(planes, axis=2)
    n, rows, _ = lhs.shape
    r = jnp.dot(lhs.reshape(n * rows, 768), w1_ref[...], preferred_element_type=F32)
    return r.reshape(n, rows, 768)


def sums_1(own, q):
    own = own.reshape(-1, 768)
    row1 = jnp.sum(own, axis=0, keepdims=True)
    row2 = jnp.sum(own * own, axis=0, keepdims=True)
    at = iota((1, 768), 1)
    if q == 0:
        row1, row2 = (jnp.where(at >= 128, r_, 0.0) for r_ in (row1, row2))
    if q == 2:
        row1, row2 = (jnp.where(at < 640, r_, 0.0) for r_ in (row1, row2))
    return row1, row2


def halve_rows(r, rows, half_ref, q):
    n = r.shape[0]
    flat = r.reshape(n * 48, 768)
    for j in range(6):
        rows[j, 0 : n * 48] = flat[:, j * 128 : (j + 1) * 128]
    for j in range(6):
        half_ref[q * 6 + j] = paired_rows(rows, j, n * 24)


def widen_kernel(volume_ref, inner_ref, outer_ref, wide_ref, outer_face_ref):
    odd = lax.axis_index("gz") % 2
    volume, inner, outer = (ref[...].astype(F32) for ref in (volume_ref, inner_ref, outer_ref))
    edge = jnp.where((iota((8, 32, 128), 2) < 64) == (odd == 0), inner, outer)
    wide = jnp.concatenate([volume, edge], axis=2)
    wide_ref[...] = wide.astype(BF16)
    core = lax.axis_index("gc")
    outer_face_ref[...] = jnp.where(core == 0, wide[:, 0:8], wide[:, 24:32]).astype(BF16)


def widen(volume, inner, outer):
    return call(
        widen_kernel,
        [near((8, 32, 256), BF16), near((8, 8, 256), BF16)],
        [(volume, VMEM), (inner, VMEM), (outer, VMEM)],
    )


def inner_face_kernel(wide_ref, face_ref):
    wide = wide_ref[...].astype(F32)
    face_ref[...] = jnp.where(lax.axis_index("gc") == 0, wide[:, 24:32], wide[:, 0:8]).astype(BF16)


def inner_face(wide):
    cost = pl.CostEstimate(flops=0, bytes_accessed=8_000_000, transcendentals=0)
    return call(inner_face_kernel, [near((8, 8, 256), BF16)], [(wide, VMEM)], cost=cost)[0]


def assemble_kernel(wide_ref, inner_ref, outer_ref, mid_ref, inner_out, outer_out):
    core = lax.axis_index("gc")
    inner, outer = inner_ref[...].astype(F32), outer_ref[...].astype(F32)
    low = jnp.where(core == 0, outer, inner)
    high = jnp.where(core == 0, inner, outer)
    mid = jnp.concatenate([low, wide_ref[...].astype(F32), high], axis=1)
    mid_ref[...] = mid.astype(BF16)
    slot = (iota((48, 128), 1) + 8) % 128 // 16
    ends = mid[0, :, 128:256]
    for i in range(1, 8):
        ends = jnp.where(slot == i, pltpu.roll(mid[i, :, 128:256], 16 * i, 1), ends)
    even = lax.axis_index("gx") % 2 == 0
    lower, upper = mid[0:7, :, 0:128], mid[1:8, :, 0:128]
    inner_out[0:7] = jnp.where(even, upper, lower).astype(BF16)
    outer_out[0:7] = jnp.where(even, lower, upper).astype(BF16)
    inner_out[7] = ends.astype(BF16)
    outer_out[7] = ends.astype(BF16)


def assemble(wide, inner, outer):
    return call(
        assemble_kernel,
        [near((8, 48, 256), BF16), near((8, 48, 128), BF16), near((8, 48, 128), BF16)],
        [(wide, VMEM), (inner, VMEM), (outer, VMEM)],
    )


def plane(own, ends, i):
    ends = ends.astype(F32)
    if i:
        ends = pltpu.roll(ends, 128 - 16 * i, 1)
    return jnp.concatenate([own.astype(F32), ends], axis=1)


def middle_kernel(mid_ref, w1_ref, lhs_ref, far_ref, sums_ref):
    for i in range(8):
        fill(lhs_ref, i, mid_ref[i].astype(F32))
    far_ref[...] = lhs_ref[...]
    s1 = jnp.zeros((1, 768), F32)
    s2 = jnp.zeros((1, 768), F32)
    for q in range(3):
        r = response_1([lhs_ref[q, dx : 6 + dx][:, 8:40] for dx in range(3)], w1_ref)
        row1, row2 = sums_1(r, q)
        s1, s2 = s1 + row1, s2 + row2
    sums_ref[0:1, :] = s1
    sums_ref[1:2, :] = s2


def middle_part(mid, w1):
    return call(
        middle_kernel,
        [near((3, 8, 48, 256), BF16), far((3, 8, 48, 256), BF16), near((8, 768), F32)],
        [(mid, VMEM), (w1, VMEM)],
    )


def first_kernel(inner_ref, outer_ref, mid_ref, sums_ref, w1_ref, ends_ref, sides_ref, stats_ref):
    even = lax.axis_index("gx") % 2 == 0

    @pl.when(even)
    def _():
        sides_ref[0] = outer_ref[...]
        sides_ref[1] = inner_ref[...]

    @pl.when(jnp.logical_not(even))
    def _():
        sides_ref[0] = inner_ref[...]
        sides_ref[1] = outer_ref[...]

    fill(ends_ref, 0, plane(sides_ref[0, 6], sides_ref[0, 7], 7))
    fill(ends_ref, 1, plane(sides_ref[1, 0], sides_ref[1, 7], 0))
    planes = []
    for q in range(3):
        a = [ends_ref[q, 0:1], mid_ref[q, 0:1], mid_ref[q, 1:2]]
        b = [mid_ref[q, 6:7], mid_ref[q, 7:8], ends_ref[q, 1:2]]
        planes.append([jnp.concatenate([a[dx], b[dx]], axis=0)[:, 8:40] for dx in range(3)])
    r = response_1([jnp.concatenate([planes[q][dx] for q in range(3)], axis=0) for dx in range(3)], w1_ref)
    s1 = sums_ref[0:1, :]
    s2 = sums_ref[1:2, :]
    for q in range(3):
        row1, row2 = sums_1(r[2 * q : 2 * q + 2], q)
        s1, s2 = s1 + row1, s2 + row2
    stats_ref[...] = slots(pack_stats(s1, s2, 16))


def first_part(inner, outer, lhs_mid, sums, w1):
    return call(
        first_kernel,
        [far((3, 2, 48, 256), BF16), far((2, 8, 48, 128), BF16), far((DEVICES, 1, 128), F32)],
        [(inner, VMEM), (outer, VMEM), (lhs_mid, VMEM), (sums, VMEM), (w1, VMEM)],
    )


def wide_first_kernel(sides_ref, mid_far, ends_far, w1_far, half_ref, lhs, rows, w1_ref, sems):
    copies = [pltpu.make_async_copy(w1_far, w1_ref, sems.at[0])]
    for q in range(3):
        copies.append(pltpu.make_async_copy(mid_far.at[q], lhs.at[q, 7:15], sems.at[3 * q + 1]))
        copies.append(pltpu.make_async_copy(ends_far.at[q, 0], lhs.at[q, 6], sems.at[3 * q + 2]))
        copies.append(pltpu.make_async_copy(ends_far.at[q, 1], lhs.at[q, 15], sems.at[3 * q + 3]))
    for c in copies:
        c.start()
    for i in range(6):
        fill(lhs, i, plane(sides_ref[0, i], sides_ref[0, 7], 1 + i))
        fill(lhs, 16 + i, plane(sides_ref[1, 1 + i], sides_ref[1, 7], 1 + i))
    for c in copies:
        c.wait()
    for q in range(3):
        r = response_1([lhs[q, dx : 20 + dx] for dx in range(3)], w1_ref)
        r = jnp.max(r.reshape(10, 2, 48, 768), axis=1).reshape(480, 768)
        for j in range(6):
            rows[j] = r[:, j * 128 : (j + 1) * 128]
        for j in range(6):
            half_ref[q * 6 + j] = paired_rows(rows, j, 240)


def wide_first_part(sides, lhs_mid, ends, w1):
    return call(
        wide_first_kernel,
        [near((18, 240, 128), F32)],
        [(held(sides), VMEM)] + [(held(a), ANY) for a in (lhs_mid, ends, w1)],
        [((3, 22, 48, 256), BF16), ((6, 480, 128), F32), ((768, 768), BF16), pltpu.SemaphoreType.DMA((10,))],
    )[0]


def first_output_kernel(mid_ref, ends_ref, w1_ref, stats_ref, params_ref, f1_ref):
    normal = normaliser(jnp.sum(stats_ref[...], axis=0), VOXELS_1, params_ref, 0, 6)
    for q in range(3):
        middle = mid_ref[q]
        planes = [
            jnp.concatenate([ends_ref[q, 0:1], middle[0:7]], axis=0),
            middle,
            jnp.concatenate([middle[1:8], ends_ref[q, 1:2]], axis=0),
        ]
        f = settle(response_1([p[:, 8:40, :] for p in planes], w1_ref), normal)
        a, b = (128 if q == 0 else 0), (640 if q == 2 else 768)
        f1_ref[:, :, q * 768 - 128 + a : q * 768 - 128 + b] = f[:, :, a:b].astype(BF16)


def first_output(lhs_mid, ends, w1, stats, table):
    return call(
        first_output_kernel,
        [full((8, 32, 2048), BF16)],
        [(held(a), VMEM) for a in (lhs_mid, ends, w1)] + [(stats, VMEM), (table, VMEM)],
    )[0]


def selector(chans):
    row, col = iota((256, 256), 0), iota((256, 256), 1)
    return (row == (col % 128) // chans * (2 * chans) + col % chans + col // 128 * chans).astype(BF16)


def halved(left, right, normal, pick):
    features = jnp.concatenate([settle(left, normal), settle(right, normal)], axis=1).astype(BF16)
    both = jnp.dot(features, pick, preferred_element_type=F32)
    return jnp.maximum(both[:, 0:128], both[:, 128:256])


def second_kernel(half_ref, stats_ref, params_ref, w2_ref, p1_far, out_stats_ref, p1, p1_ref, pd, sem):
    normal = normaliser(jnp.sum(stats_ref[...], axis=0), VOXELS_1, params_ref, 0, 1)
    pick = selector(16)
    bx, by, bz = position()
    p1[:, :, 1152:1280] = jnp.zeros((10, 24, 128), F32)
    gy = iota((10, 24, 128), 1) - 4 + by * 16
    gx = iota((10, 24, 128), 0) - 3 + bx * 4
    inside = (gy >= 0) & (gy < 64) & (gx >= 0) & (gx < 32)
    for j in range(9):
        pooled = halved(half_ref[2 * j], half_ref[2 * j + 1], normal, pick).reshape(10, 24, 128)
        gz = iota((10, 24, 128), 2) // 16 - 4 + 8 * j + bz * 64
        p1[:, :, j * 128 : (j + 1) * 128] = jnp.where(inside & (gz >= 0) & (gz < 256), pooled, 0.0)
    for dy in range(3):
        pd[dy] = p1[2:8, 3 + dy : 19 + dy, :].astype(BF16)
    p1_ref[...] = p1[...].astype(BF16)
    save = pltpu.make_async_copy(p1_ref, p1_far, sem)
    save.start()
    planes = []
    for dx in range(3):
        for dy in range(3):
            pieces = [pd[dy, dx : dx + 4, :, 128 * t : 128 * t + 256].reshape(64, 256) for t in range(9)]
            planes.append(jnp.concatenate(pieces, axis=0))
    r = jnp.dot(jnp.concatenate(planes, axis=1), w2_ref[...], preferred_element_type=F32)
    s1 = jnp.zeros((1, 256), F32)
    s2 = jnp.zeros((1, 256), F32)
    lane = iota((1, 256), 1)
    for t in range(9):
        own = r[64 * t : 64 * t + 64]
        row1 = jnp.sum(own, axis=0, keepdims=True)
        row2 = jnp.sum(own * own, axis=0, keepdims=True)
        if t == 0:
            row1, row2 = (jnp.where(lane >= 64, r_, 0.0) for r_ in (row1, row2))
        if t == 8:
            row1, row2 = (jnp.where(lane < 64, r_, 0.0) for r_ in (row1, row2))
        s1, s2 = s1 + row1, s2 + row2
    out_stats_ref[...] = slots(pack_stats(s1, s2, 32))
    save.wait()


def second_part(half, stats, table, w2):
    return call(
        second_kernel,
        [far((10, 24, 1280), BF16), far((DEVICES, 1, 128), F32)],
        [(a, VMEM) for a in (half, stats, table, w2)],
        [((10, 24, 1280), F32), ((10, 24, 1280), BF16), ((3, 6, 16, 1280), BF16), pltpu.SemaphoreType.DMA(())],
        [ANY, VMEM],
    )


def wide_second_kernel(p1_ref, w2_ref, k3_far, half_ref, r2_ref, w3_ref, pd, rows, k3_ref, t_ref, sem):
    kernel = pltpu.make_async_copy(k3_far, k3_ref, sem)
    kernel.start()

    def shift(i, carry):
        v = p1_ref[i].astype(F32)
        pd[0, i] = pltpu.roll(v, 1, 0)
        pd[1, i] = v
        pd[2, i] = pltpu.roll(v, 23, 0)
        return carry

    lax.fori_loop(0, 10, shift, 0)
    for t in range(0, 9, 3):
        planes = []
        for dx in range(3):
            for dy in range(3):
                pieces = [pd[dy, dx : dx + 8, :, 128 * u : 128 * u + 256].reshape(192, 256) for u in range(t, t + 3)]
                planes.append(jnp.concatenate(pieces, axis=0).astype(BF16))
        r = jnp.dot(jnp.concatenate(planes, axis=1), w2_ref[...], preferred_element_type=F32)
        own = r.reshape(3, 8, 24, 256)[:, 2:6, 4:20]
        r2_ref[64 * t : 64 * t + 192, :] = own.reshape(192, 256)
        r = jnp.max(r.reshape(3, 4, 2, 24, 256), axis=2).reshape(3, 96, 256)
        for i in range(3):
            for j in range(2):
                rows[2 * i + j] = r[i, :, j * 128 : (j + 1) * 128]
        for j in range(6):
            half_ref[2 * t + j] = paired_rows(rows, j, 48)
    kernel.wait()
    band_kernel(32, 64, 0, k3_ref, w3_ref, t_ref)


def wide_second_part(p1, w2, k3):
    return call(
        wide_second_kernel,
        [near((18, 48, 128), F32), far((576, 256), F32), near((2304, 256), BF16)],
        [(held(p1), VMEM), (w2, VMEM), (held(k3.reshape(864, 64)), ANY)],
        [((3, 10, 24, 1280), F32), ((6, 96, 128), F32), ((864, 64), BF16), ((864, 256), F32)]
        + [pltpu.SemaphoreType.DMA(())],
    )


def second_output_kernel(r2_ref, stats_ref, params_ref, f2_ref):
    normal = normaliser(jnp.sum(stats_ref[...], axis=0), VOXELS_1 / 8, params_ref, 1, 2)
    f = [settle(r2_ref[64 * t : 64 * t + 64, :], normal) for t in range(9)]
    wide = pltpu.roll(jnp.concatenate(f, axis=1), 2304 - 64, 1)[:, 0:2048]
    f2_ref[...] = wide.reshape(4, 16, 2048).astype(BF16)


def second_output(r2, stats, table):
    return call(
        second_output_kernel,
        [full((4, 16, 2048), BF16)],
        [(held(r2), VMEM), (stats, VMEM), (table, VMEM)],
    )[0]


def third_kernel(half_ref, stats_ref, params_ref, w3_ref, r3_ref, out_ref, p2, yrow):
    normal = normaliser(jnp.sum(stats_ref[...], axis=0), VOXELS_1 / 8, params_ref, 1, 1)
    bx, by, bz = position()
    pick = selector(32)
    gy = iota((12, 128), 0) - 2 + by * 8
    for j in range(9):
        pooled = halved(half_ref[2 * j], half_ref[2 * j + 1], normal, pick)
        gz = iota((12, 128), 1) // 32 + 4 * j - 1 + bz * 32
        inside = (gy >= 0) & (gy < 32) & (gz >= 0) & (gz < 128)
        for px in range(4):
            gx = px - 1 + bx * 2
            p2[px, 0:12, j * 128 : (j + 1) * 128] = jnp.where(
                inside & (gx >= 0) & (gx < 16), pooled[px * 12 : px * 12 + 12, :], 0.0
            )
    planes = []
    for dx in range(3):
        for dy in range(3):
            pieces = []
            for t in range(8):
                for x in range(2):
                    pieces.append(p2[x + dx, 1 + dy : 9 + dy, 128 * t : 128 * t + 256])
            planes.append(jnp.concatenate(pieces, axis=0).astype(BF16))
    r = jnp.dot(jnp.concatenate(planes, axis=1), w3_ref[...], preferred_element_type=F32)
    r3_ref[...] = r
    s1 = fold(jnp.sum(r, axis=0, keepdims=True), 64)
    s2 = fold(jnp.sum(r * r, axis=0, keepdims=True), 64)
    low = iota((8, 128), 1) < 64
    for t in range(8):
        m = jnp.maximum(r[t * 16 : t * 16 + 8, :], r[t * 16 + 8 : t * 16 + 16, :])
        a, b = m[:, 0:128], m[:, 128:256]
        a = jnp.maximum(a, pltpu.roll(a, 64, 1))
        b = jnp.maximum(b, pltpu.roll(b, 64, 1))
        yrow[:, t * 128 : (t + 1) * 128] = jnp.where(low, a, b)
    pooled = jnp.concatenate(
        [jnp.maximum(yrow[2 * i : 2 * i + 1, :], yrow[2 * i + 1 : 2 * i + 2, :]) for i in range(4)], axis=0
    )
    mean_here = s1 / 512.0
    spread = jnp.sqrt(jnp.maximum(s2 / 512.0 - mean_here * mean_here, 0.0))
    begin = mean_here + jnp.clip(-params_ref[5:6, :] / params_ref[4:5, :], -8.0, 8.0) * spread
    offset = jnp.maximum(begin, fold(jnp.sum(pooled, axis=0, keepdims=True), 64) / 64.0)
    at = iota((1, 128), 1)
    offset = offset.astype(BF16).astype(F32)
    apart = pooled - jnp.concatenate([offset] * 8, axis=1)
    wide = pltpu.roll(jnp.concatenate([apart, jnp.zeros((4, 128), F32)], axis=1), 64, 1)
    sums = jnp.where(at < 64, s1, s2)
    high = sums.astype(BF16).astype(F32)
    middle = (sums - high).astype(BF16).astype(F32)
    edge = jnp.concatenate([high, middle, sums - high - middle, offset], axis=0)
    ends = iota((4, 128), 1) < 64
    out = jnp.concatenate(
        [jnp.where(ends, edge, wide[:, 0:128]), wide[:, 128:1024], jnp.where(ends, wide[:, 1024:1152], edge)], axis=1
    ).astype(BF16)
    out_ref[...] = jnp.broadcast_to(out.reshape(1, 4, 1152), (DEVICES // 2, 4, 1152))


def third_part(half, stats, table, w3):
    return call(
        third_kernel,
        [near((128, 256), F32), far((DEVICES // 2, 4, 1152), BF16)],
        [(a, VMEM) for a in (half, stats, table, w3)],
        [((4, 16, 1152), F32), ((8, 1024), F32)],
    )


def fourth_kernel(r3_ref, own_ref, other_ref, params_ref, w4_ref, f3_ref, out_far, p3, pd, r4, out_ref, sems):
    edge = jnp.zeros((4, 128), F32)
    tail = jnp.zeros((4, 128), F32)
    for ref in (own_ref, other_ref):
        edge = edge + jnp.sum(ref[:, :, 0:128].astype(F32), axis=0)
        tail = tail + jnp.sum(ref[:, :, 1024:1152].astype(F32), axis=0)
    total = jnp.sum(jnp.where(iota((4, 128), 1) < 64, edge, tail)[0:3, :], axis=0, keepdims=True)
    normal = normaliser(total, VOXELS_1 / 64, params_ref, 2, 2)
    f3 = settle(r3_ref[...], normal)
    for t in range(8):
        for x in range(2):
            f3_ref[x, :, t * 256 : (t + 1) * 256] = f3[t * 16 + x * 8 : t * 16 + x * 8 + 8, :].astype(BF16)
    lane = iota((4, 128), 1)
    low = iota((16, 128), 1) < 64
    y = iota((16, 128), 0)
    one = tuple(v[:, 0:128] for v in normal)
    zero = jnp.zeros((16, 4224), BF16)
    for dy in range(3):
        pd[dy, 0] = zero
        pd[dy, 9] = zero

    first_core = lax.axis_index("gc") == 0

    def place(gx):
        for gh in range(2):
            last = [jnp.zeros((4, 128), F32)] * 2
            for gz in range(4):
                block = (gx * 2 + gh) * 4 + gz
                mine, theirs = own_ref[block].astype(F32), other_ref[block].astype(F32)
                start = gz * 1024
                for gc, v in enumerate((jnp.where(first_core, mine, theirs), jnp.where(first_core, theirs, mine))):
                    y0 = 8 * gh + 4 * gc
                    v0, v8 = v[:, 0:128], v[:, 1024:1152]
                    offset = jnp.where(lane < 64, v0, v8)[3:4, :]
                    p3[gx % 2, y0 : y0 + 4, start : start + 128] = jnp.where(lane < 64, last[gc], v0 + offset)
                    p3[gx % 2, y0 : y0 + 4, start + 128 : start + 1024] = v[:, 128:1024] + jnp.concatenate([offset] * 7, axis=1)
                    last[gc] = v8 + offset
            for gc in range(2):
                p3[gx % 2, 8 * gh + 4 * gc : 8 * gh + 4 * gc + 4, 4096:4224] = last[gc]
        for j in range(33):
            lanes = slice(j * 128, (j + 1) * 128)
            v = settle(p3[gx % 2, :, lanes], one)
            if j == 0:
                v = jnp.where(low, 0.0, v)
            if j == 32:
                v = jnp.where(low, v, 0.0)
            pd[0, gx + 1, :, lanes] = jnp.where(y > 0, pltpu.roll(v, 1, 0), 0.0).astype(BF16)
            pd[1, gx + 1, :, lanes] = v.astype(BF16)
            pd[2, gx + 1, :, lanes] = jnp.where(y < 15, pltpu.roll(v, 15, 0), 0.0).astype(BF16)

    def multiply(x0, count, t0, tiles, sums):
        planes = []
        for dx in range(3):
            for dy in range(3):
                pieces = [
                    pd[dy, x0 + dx : x0 + dx + count, :, 128 * t : 128 * t + 256].reshape(count * 16, 256)
                    for t in range(t0, t0 + tiles)
                ]
                planes.append(jnp.concatenate(pieces, axis=0))
        r = jnp.dot(jnp.concatenate(planes, axis=1), w4_ref[...], preferred_element_type=F32)
        for i in range(tiles):
            at = (t0 + i) * 128 + x0 * 16
            r4[at : at + count * 16, :] = r[i * count * 16 : (i + 1) * count * 16]
        return sums[0] + jnp.sum(r, axis=0, keepdims=True), sums[1] + jnp.sum(r * r, axis=0, keepdims=True)

    sums = (jnp.zeros((1, 256), F32), jnp.zeros((1, 256), F32))
    for gx in range(8):
        place(gx)
        if gx % 2 == 0 and gx:
            for t in (0, 16):
                sums = multiply(gx - 2, 2, t, 16, sums)
    for t in (0, 16):
        sums = multiply(6, 2, t, 16, sums)
    s1, s2 = sums
    cells = VOXELS_1 / 512
    mean = fold(s1, 128) / cells
    variance = fold(s2, 128) / cells - mean * mean
    factor = params_ref[6:7, :] * lax.rsqrt(variance + EPSILON)
    last = tuple(jnp.concatenate([v] * 2, axis=1) for v in (mean, factor, params_ref[7:8, :]))

    copies = []
    for i in range(4):
        for t in range(8 * i, 8 * i + 8):
            f = settle(r4[t * 128 : t * 128 + 128, :], last).astype(BF16)
            out_ref[:, :, 256 * t : 256 * t + 256] = f.reshape(8, 16, 256)
        lanes = pl.ds(2048 * i, 2048)
        copies.append(pltpu.make_async_copy(out_ref.at[:, :, lanes], out_far.at[:, :, lanes], sems.at[i]))
        copies[i].start()
    for c in copies:
        c.wait()


def fourth_part(r3, own, other, table, w4):
    return call(
        fourth_kernel,
        [full((2, 8, 2048), BF16), far((8, 16, 8192), BF16)],
        [(a, VMEM) for a in (r3, own, other, table, w4)],
        [((2, 16, 4224), F32), ((3, 10, 16, 4224), BF16), ((4096, 256), F32), ((8, 16, 8192), BF16)]
        + [pltpu.SemaphoreType.DMA((4,))],
        [VMEM, ANY],
    )


def across(block, axis, swaps):
    return lax.ppermute(block, axis, swaps + [(b, a) for a, b in swaps])


def after(values, event):
    return lax.optimization_barrier((values, event))


def shards(volume, k1, g1, b1, k2, g2, b2, k3, g3, b3, k4, g4, b4):
    outer = across(volume, "gz", [(1, 2)])
    inner = across(volume, "gz", [(0, 1), (2, 3)])
    w1, w1_far, block = first_band(k1, volume)
    (inner, outer, w1) = lax.optimization_barrier((inner, outer, w1))
    wide, outer = widen(block, inner, outer)
    (wide, outer, k2) = lax.optimization_barrier((wide, outer, k2))
    outer = across(outer, ("gh", "gc"), [(1, 2)])
    inner = across(inner_face(wide), "gc", [(0, 1)])
    mid, inner, outer = assemble(wide, inner, outer)
    (mid, k2) = lax.optimization_barrier((mid, k2))
    inner = across(inner, "gx", [(0, 1), (2, 3), (4, 5), (6, 7)])
    outer = across(outer, "gx", [(1, 2), (3, 4), (5, 6)])
    w2, table = early_part(k2, (g1, b1, g2, b2, g3, b3, g4, b4))
    lhs_mid, far_mid, sums = middle_part(mid, w1)
    (inner, outer, lhs_mid, w2) = lax.optimization_barrier((inner, outer, lhs_mid, w2))
    ends, sides, stats = first_part(inner, outer, lhs_mid, sums, w1)

    total1 = lax.all_to_all(stats, AXES, 0, 0, tiled=True)
    half1 = wide_first_part(sides, far_mid, ends, w1_far)
    half1, total1 = after(half1, total1)
    p1, stats = second_part(half1, total1, table, w2)

    p1, stats = after(p1, stats)
    total2 = lax.all_to_all(stats, AXES, 0, 0, tiled=True)
    half2, r2, w3 = wide_second_part(p1, w2, k3)
    (half2, w3), total2 = after((half2, w3), total2)
    r3, packed = third_part(half2, total2, table, w3)

    (k4, far_mid, r2), packed = after((k4, far_mid, r2), packed)
    own = lax.all_to_all(packed, CHIPS, 0, 0, tiled=True)
    f1 = first_output(far_mid, ends, w1_far, total1, table)
    f2 = second_output(r2, total2, table)
    w4 = band(k4, 0)
    (f1, f2, w4), own = after((f1, f2, w4), own)
    other = lax.ppermute(own, "gc", [(0, 1), (1, 0)])
    f3, f4 = fourth_part(r3, own, other, table, w4)
    return f1, f2, f3, f4


def solution(mesh):
    parts = Mesh(mesh.devices.reshape(8, 2, 2, 4), AXES)
    spread = P("gx", ("gh", "gc"), "gz")
    return jax.shard_map(
        shards,
        mesh=parts,
        in_specs=(spread,) + (P(),) * 12,
        out_specs=(spread, spread, spread, P()),
        check_vma=False,
    )
```

```python
import functools

import jax
import jax.numpy as jnp
from jax import lax
from jax.experimental import pallas as pl
from jax.experimental.pallas import tpu as pltpu
from jax.sharding import Mesh
from jax.sharding import PartitionSpec as P

EPSILON = 1e-05
F32 = jnp.float32
BF16 = jnp.bfloat16
AXES = ("gx", "gh", "gc", "gz")
CHIPS = ("gx", "gh", "gz")
DEVICES = 128
VOXELS_1 = 64.0 * 128.0 * 512.0
PARAMS = pltpu.CompilerParams(vmem_limit_bytes=40 * 1024 * 1024)


def full(shape, dtype):
    return jax.ShapeDtypeStruct(shape, dtype)


def iota(shape, dim):
    return lax.broadcasted_iota(jnp.int32, shape, dim)


VMEM = pl.BlockSpec(memory_space=pltpu.VMEM)
ANY = pl.BlockSpec(memory_space=pl.ANY)


def near(shape, dtype):
    return pltpu.VMEM(shape, dtype)


def far(shape, dtype):
    return pltpu.HBM(shape, dtype)


def held(array):
    return pltpu.with_memory_space_constraint(array, pltpu.HBM)


def call(kernel, outs, ins, scratch=(), out_specs=None, cost=None):
    return pl.pallas_call(
        kernel,
        in_specs=[spec for _, spec in ins],
        out_specs=tuple(out_specs or [VMEM] * len(outs)),
        out_shape=tuple(outs),
        scratch_shapes=[s if not isinstance(s, tuple) else pltpu.VMEM(*s) for s in scratch],
        compiler_params=PARAMS,
        cost_estimate=cost,
    )(*[array for array, _ in ins])


def position():
    gx, gh, gc, gz = (lax.axis_index(a) for a in AXES)
    return gx, gh * 2 + gc, gz


def first_band_kernel(k_ref, volume_far, w_ref, far_ref, volume_ref, sem):
    own = pltpu.make_async_copy(volume_far, volume_ref, sem)
    own.start()
    spread = (iota((16, 768), 1) % 16 == iota((16, 768), 0)).astype(BF16)
    taps = jnp.dot(k_ref[...], spread, preferred_element_type=F32)
    lag = iota((64, 768), 0) - iota((64, 768), 1) // 16
    for dx in range(3):
        for dy in range(3):
            block = jnp.zeros((64, 768), F32)
            for dz in range(3):
                t = (dx * 3 + dy) * 3 + dz
                block = jnp.where(lag == dz, taps[t : t + 1, :], block)
            w_ref[dx * 256 + dy * 64 : dx * 256 + dy * 64 + 64, :] = block.astype(BF16)
        w_ref[dx * 256 + 192 : dx * 256 + 256, :] = jnp.zeros((64, 768), BF16)
    far_ref[...] = w_ref[...]
    own.wait()


def fill_params(vectors, out_ref):
    lane = iota((1, 128), 1)
    for i, ref in enumerate(vectors):
        count = ref.shape[0]
        row = jnp.zeros((1, 128), F32)
        for c in range(count):
            row = jnp.where(lane % count == c, ref[c], row)
        out_ref[i : i + 1, :] = row


def band_kernel(cin, cout, first, k_ref, w_ref, t_ref):
    outs = 256 // cout
    tile = (iota((cout, 256), 1) % cout == iota((cout, 256), 0)).astype(BF16)
    t_ref[...] = jnp.dot(k_ref[...], tile, preferred_element_type=F32)
    zo = iota((cin, 256), 1) // cout

    def plane(p, carry):
        for zi in range(-first, 256 // cin - first):
            block = jnp.zeros((cin, 256), F32)
            if 0 <= zi < outs + 2:
                for dz in range(3):
                    start = pl.multiple_of((p * 3 + dz) * cin, cin)
                    block = jnp.where(zo == zi - dz, t_ref[pl.ds(start, cin), :], block)
            start = pl.multiple_of(p * 256 + (zi + first) * cin, cin)
            w_ref[pl.ds(start, cin), :] = block.astype(BF16)
        return carry

    lax.fori_loop(0, 9, plane, 0)


def first_band(k, volume):
    return call(
        first_band_kernel,
        [near((768, 768), BF16), far((768, 768), BF16), near(volume.shape, BF16)],
        [(k.reshape(27, 16), VMEM), (held(volume), ANY)],
        [pltpu.SemaphoreType.DMA(())],
    )


def early_kernel(*refs):
    k2_far, vectors_far = refs[0], refs[1:9]
    w2_ref, params_ref, k2_ref, t_ref = refs[9:13]
    vectors, sems = refs[13:21], refs[21]
    copies = [pltpu.make_async_copy(k2_far, k2_ref, sems.at[8])]
    copies += [pltpu.make_async_copy(v, p, sems.at[i]) for i, (v, p) in enumerate(zip(vectors_far, vectors))]
    for c in copies:
        c.start()
    for c in copies:
        c.wait()
    band_kernel(16, 32, 1, k2_ref, w2_ref, t_ref)
    fill_params(vectors, params_ref)


def early_part(k2, vectors):
    return call(
        early_kernel,
        [near((2304, 256), BF16), near((8, 128), F32)],
        [(held(k2.reshape(432, 32)), ANY)] + [(held(v), ANY) for v in vectors],
        [((432, 32), BF16), ((432, 256), F32)]
        + [pltpu.SMEM(v.shape, F32) for v in vectors]
        + [pltpu.SemaphoreType.DMA((9,))],
    )


def band(k, first):
    cin, cout = k.shape[3:]
    return call(
        functools.partial(band_kernel, cin, cout, first),
        [near((2304, 256), BF16)],
        [(held(k.reshape(27 * cin, cout)), VMEM)],
        [((27 * cin, 256), F32)],
    )[0]


def fold(row, width):
    total = row[:, 0:128]
    for j in range(1, row.shape[1] // 128):
        total = total + row[:, j * 128 : (j + 1) * 128]
    step = 64
    while step >= width:
        total = total + pltpu.roll(total, step, 1)
        step //= 2
    return total


def pack_stats(s1, s2, width):
    return jnp.where(iota((1, 128), 1) < 64, fold(s1, width), fold(s2, width))


def normaliser(total, cells, params_ref, level, copies):
    lane = iota((1, 128), 1)
    other = pltpu.roll(total, 64, 1)
    mean = jnp.where(lane < 64, total, other) / cells
    variance = jnp.where(lane < 64, other, total) / cells - mean * mean
    shift = params_ref[2 * level + 1 : 2 * level + 2, :]
    factor = params_ref[2 * level : 2 * level + 1, :] * lax.rsqrt(variance + EPSILON)
    return tuple(jnp.concatenate([v] * copies, axis=1) for v in (mean, factor, shift))


def settle(response, normal):
    mean, factor, shift = normal
    return jnp.maximum((response - mean) * factor + shift, 0.0)


def slots(stats):
    return jnp.broadcast_to(stats.reshape(1, 1, 128), (DEVICES, 1, 128))


def paired_rows(ref, j, count):
    return jnp.maximum(ref[j, pl.ds(0, count, stride=2), :], ref[j, pl.ds(1, count, stride=2), :])


def fill(out_ref, at, v):
    lane = iota((48, 128), 1)
    for q, part, turn in ((0, v, 9), (1, v[:, 0:128], 128 - 39), (2, v, 256 - 87)):
        wa = pltpu.roll(part, turn, 1)[:, 0:128]
        wb = pltpu.roll(wa, 64, 1)
        out_ref[q, at, :, 0:128] = jnp.where(lane < 64, pltpu.roll(wa, 1, 0), wb).astype(BF16)
        out_ref[q, at, :, 128:256] = pltpu.roll(wa, 47, 0).astype(BF16)


def response_1(planes, w1_ref):
    lhs = jnp.concatenate(planes, axis=2)
    n, rows, _ = lhs.shape
    r = jnp.dot(lhs.reshape(n * rows, 768), w1_ref[...], preferred_element_type=F32)
    return r.reshape(n, rows, 768)


def sums_1(own, q):
    own = own.reshape(-1, 768)
    row1 = jnp.sum(own, axis=0, keepdims=True)
    row2 = jnp.sum(own * own, axis=0, keepdims=True)
    at = iota((1, 768), 1)
    if q == 0:
        row1, row2 = (jnp.where(at >= 128, r_, 0.0) for r_ in (row1, row2))
    if q == 2:
        row1, row2 = (jnp.where(at < 640, r_, 0.0) for r_ in (row1, row2))
    return row1, row2


def halve_rows(r, rows, half_ref, q):
    n = r.shape[0]
    flat = r.reshape(n * 48, 768)
    for j in range(6):
        rows[j, 0 : n * 48] = flat[:, j * 128 : (j + 1) * 128]
    for j in range(6):
        half_ref[q * 6 + j] = paired_rows(rows, j, n * 24)


def widen_kernel(volume_ref, inner_ref, outer_ref, wide_ref, outer_face_ref):
    odd = lax.axis_index("gz") % 2
    volume, inner, outer = (ref[...].astype(F32) for ref in (volume_ref, inner_ref, outer_ref))
    edge = jnp.where((iota((8, 32, 128), 2) < 64) == (odd == 0), inner, outer)
    wide = jnp.concatenate([volume, edge], axis=2)
    wide_ref[...] = wide.astype(BF16)
    core = lax.axis_index("gc")
    outer_face_ref[...] = jnp.where(core == 0, wide[:, 0:8], wide[:, 24:32]).astype(BF16)


def widen(volume, inner, outer):
    return call(
        widen_kernel,
        [near((8, 32, 256), BF16), near((8, 8, 256), BF16)],
        [(volume, VMEM), (inner, VMEM), (outer, VMEM)],
    )


def inner_face_kernel(wide_ref, face_ref):
    wide = wide_ref[...].astype(F32)
    face_ref[...] = jnp.where(lax.axis_index("gc") == 0, wide[:, 24:32], wide[:, 0:8]).astype(BF16)


def inner_face(wide):
    cost = pl.CostEstimate(flops=0, bytes_accessed=8_000_000, transcendentals=0)
    return call(inner_face_kernel, [near((8, 8, 256), BF16)], [(wide, VMEM)], cost=cost)[0]


def assemble_kernel(wide_ref, inner_ref, outer_ref, mid_ref, inner_out, outer_out):
    core = lax.axis_index("gc")
    inner, outer = inner_ref[...].astype(F32), outer_ref[...].astype(F32)
    low = jnp.where(core == 0, outer, inner)
    high = jnp.where(core == 0, inner, outer)
    mid = jnp.concatenate([low, wide_ref[...].astype(F32), high], axis=1)
    mid_ref[...] = mid.astype(BF16)
    slot = (iota((48, 128), 1) + 8) % 128 // 16
    ends = mid[0, :, 128:256]
    for i in range(1, 8):
        ends = jnp.where(slot == i, pltpu.roll(mid[i, :, 128:256], 16 * i, 1), ends)
    even = lax.axis_index("gx") % 2 == 0
    lower, upper = mid[0:7, :, 0:128], mid[1:8, :, 0:128]
    inner_out[0:7] = jnp.where(even, upper, lower).astype(BF16)
    outer_out[0:7] = jnp.where(even, lower, upper).astype(BF16)
    inner_out[7] = ends.astype(BF16)
    outer_out[7] = ends.astype(BF16)


def assemble(wide, inner, outer):
    return call(
        assemble_kernel,
        [near((8, 48, 256), BF16), near((8, 48, 128), BF16), near((8, 48, 128), BF16)],
        [(wide, VMEM), (inner, VMEM), (outer, VMEM)],
    )


def plane(own, ends, i):
    ends = ends.astype(F32)
    if i:
        ends = pltpu.roll(ends, 128 - 16 * i, 1)
    return jnp.concatenate([own.astype(F32), ends], axis=1)


def middle_kernel(mid_ref, w1_ref, lhs_ref, far_ref, sums_ref):
    for i in range(8):
        fill(lhs_ref, i, mid_ref[i].astype(F32))
    far_ref[...] = lhs_ref[...]
    s1 = jnp.zeros((1, 768), F32)
    s2 = jnp.zeros((1, 768), F32)
    for q in range(3):
        r = response_1([lhs_ref[q, dx : 6 + dx][:, 8:40] for dx in range(3)], w1_ref)
        row1, row2 = sums_1(r, q)
        s1, s2 = s1 + row1, s2 + row2
    sums_ref[0:1, :] = s1
    sums_ref[1:2, :] = s2


def middle_part(mid, w1):
    return call(
        middle_kernel,
        [near((3, 8, 48, 256), BF16), far((3, 8, 48, 256), BF16), near((8, 768), F32)],
        [(mid, VMEM), (w1, VMEM)],
    )


def first_kernel(inner_ref, outer_ref, mid_ref, sums_ref, w1_ref, ends_ref, sides_ref, stats_ref):
    even = lax.axis_index("gx") % 2 == 0

    @pl.when(even)
    def _():
        sides_ref[0] = outer_ref[...]
        sides_ref[1] = inner_ref[...]

    @pl.when(jnp.logical_not(even))
    def _():
        sides_ref[0] = inner_ref[...]
        sides_ref[1] = outer_ref[...]

    fill(ends_ref, 0, plane(sides_ref[0, 6], sides_ref[0, 7], 7))
    fill(ends_ref, 1, plane(sides_ref[1, 0], sides_ref[1, 7], 0))
    planes = []
    for q in range(3):
        a = [ends_ref[q, 0:1], mid_ref[q, 0:1], mid_ref[q, 1:2]]
        b = [mid_ref[q, 6:7], mid_ref[q, 7:8], ends_ref[q, 1:2]]
        planes.append([jnp.concatenate([a[dx], b[dx]], axis=0)[:, 8:40] for dx in range(3)])
    r = response_1([jnp.concatenate([planes[q][dx] for q in range(3)], axis=0) for dx in range(3)], w1_ref)
    s1 = sums_ref[0:1, :]
    s2 = sums_ref[1:2, :]
    for q in range(3):
        row1, row2 = sums_1(r[2 * q : 2 * q + 2], q)
        s1, s2 = s1 + row1, s2 + row2
    stats_ref[...] = slots(pack_stats(s1, s2, 16))


def first_part(inner, outer, lhs_mid, sums, w1):
    return call(
        first_kernel,
        [far((3, 2, 48, 256), BF16), far((2, 8, 48, 128), BF16), far((DEVICES, 1, 128), F32)],
        [(inner, VMEM), (outer, VMEM), (lhs_mid, VMEM), (sums, VMEM), (w1, VMEM)],
    )


def wide_first_kernel(sides_ref, mid_far, ends_far, w1_far, half_ref, lhs, rows, w1_ref, sems):
    copies = [pltpu.make_async_copy(w1_far, w1_ref, sems.at[0])]
    for q in range(3):
        copies.append(pltpu.make_async_copy(mid_far.at[q], lhs.at[q, 7:15], sems.at[3 * q + 1]))
        copies.append(pltpu.make_async_copy(ends_far.at[q, 0], lhs.at[q, 6], sems.at[3 * q + 2]))
        copies.append(pltpu.make_async_copy(ends_far.at[q, 1], lhs.at[q, 15], sems.at[3 * q + 3]))
    for c in copies:
        c.start()
    for i in range(6):
        fill(lhs, i, plane(sides_ref[0, i], sides_ref[0, 7], 1 + i))
        fill(lhs, 16 + i, plane(sides_ref[1, 1 + i], sides_ref[1, 7], 1 + i))
    for c in copies:
        c.wait()
    for q in range(3):
        r = response_1([lhs[q, dx : 20 + dx] for dx in range(3)], w1_ref)
        r = jnp.max(r.reshape(10, 2, 48, 768), axis=1).reshape(480, 768)
        for j in range(6):
            rows[j, 0:480] = r[:, j * 128 : (j + 1) * 128]
        for j in range(6):
            half_ref[q * 6 + j] = paired_rows(rows, j, 240)


def wide_first_part(sides, lhs_mid, ends, w1):
    return call(
        wide_first_kernel,
        [near((18, 240, 128), F32)],
        [(held(sides), VMEM)] + [(held(a), ANY) for a in (lhs_mid, ends, w1)],
        [((3, 22, 48, 256), BF16), ((6, 488, 128), F32), ((768, 768), BF16), pltpu.SemaphoreType.DMA((10,))],
    )[0]


def first_output_kernel(mid_ref, ends_ref, w1_ref, stats_ref, params_ref, f1_ref):
    normal = normaliser(jnp.sum(stats_ref[...], axis=0), VOXELS_1, params_ref, 0, 6)
    for q in range(3):
        middle = mid_ref[q]
        planes = [
            jnp.concatenate([ends_ref[q, 0:1], middle[0:7]], axis=0),
            middle,
            jnp.concatenate([middle[1:8], ends_ref[q, 1:2]], axis=0),
        ]
        f = settle(response_1([p[:, 8:40, :] for p in planes], w1_ref), normal)
        a, b = (128 if q == 0 else 0), (640 if q == 2 else 768)
        f1_ref[:, :, q * 768 - 128 + a : q * 768 - 128 + b] = f[:, :, a:b].astype(BF16)


def first_output(lhs_mid, ends, w1, stats, table):
    return call(
        first_output_kernel,
        [full((8, 32, 2048), BF16)],
        [(held(a), VMEM) for a in (lhs_mid, ends, w1)] + [(stats, VMEM), (table, VMEM)],
    )[0]


def selector(chans):
    row, col = iota((256, 256), 0), iota((256, 256), 1)
    return (row == (col % 128) // chans * (2 * chans) + col % chans + col // 128 * chans).astype(BF16)


def halved(left, right, normal, pick):
    features = jnp.concatenate([settle(left, normal), settle(right, normal)], axis=1).astype(BF16)
    both = jnp.dot(features, pick, preferred_element_type=F32)
    return jnp.maximum(both[:, 0:128], both[:, 128:256])


def second_kernel(half_ref, stats_ref, params_ref, w2_ref, p1_far, out_stats_ref, p1, p1_ref, pd, sem):
    normal = normaliser(jnp.sum(stats_ref[...], axis=0), VOXELS_1, params_ref, 0, 1)
    pick = selector(16)
    bx, by, bz = position()
    p1[:, :, 1152:1280] = jnp.zeros((10, 24, 128), F32)
    gy = iota((10, 24, 128), 1) - 4 + by * 16
    gx = iota((10, 24, 128), 0) - 3 + bx * 4
    inside = (gy >= 0) & (gy < 64) & (gx >= 0) & (gx < 32)
    for j in range(9):
        pooled = halved(half_ref[2 * j], half_ref[2 * j + 1], normal, pick).reshape(10, 24, 128)
        gz = iota((10, 24, 128), 2) // 16 - 4 + 8 * j + bz * 64
        p1[:, :, j * 128 : (j + 1) * 128] = jnp.where(inside & (gz >= 0) & (gz < 256), pooled, 0.0)
    for dy in range(3):
        pd[dy] = p1[2:8, 3 + dy : 19 + dy, :].astype(BF16)
    p1_ref[...] = p1[...].astype(BF16)
    save = pltpu.make_async_copy(p1_ref, p1_far, sem)
    save.start()
    planes = []
    for dx in range(3):
        for dy in range(3):
            pieces = [pd[dy, dx : dx + 4, :, 128 * t : 128 * t + 256].reshape(64, 256) for t in range(9)]
            planes.append(jnp.concatenate(pieces, axis=0))
    r = jnp.dot(jnp.concatenate(planes, axis=1), w2_ref[...], preferred_element_type=F32)
    s1 = jnp.zeros((1, 256), F32)
    s2 = jnp.zeros((1, 256), F32)
    lane = iota((1, 256), 1)
    for t in range(9):
        own = r[64 * t : 64 * t + 64]
        row1 = jnp.sum(own, axis=0, keepdims=True)
        row2 = jnp.sum(own * own, axis=0, keepdims=True)
        if t == 0:
            row1, row2 = (jnp.where(lane >= 64, r_, 0.0) for r_ in (row1, row2))
        if t == 8:
            row1, row2 = (jnp.where(lane < 64, r_, 0.0) for r_ in (row1, row2))
        s1, s2 = s1 + row1, s2 + row2
    out_stats_ref[...] = slots(pack_stats(s1, s2, 32))
    save.wait()


def second_part(half, stats, table, w2):
    return call(
        second_kernel,
        [far((10, 24, 1280), BF16), far((DEVICES, 1, 128), F32)],
        [(a, VMEM) for a in (half, stats, table, w2)],
        [((10, 24, 1280), F32), ((10, 24, 1280), BF16), ((3, 6, 16, 1280), BF16), pltpu.SemaphoreType.DMA(())],
        [ANY, VMEM],
    )


def wide_second_kernel(p1_ref, w2_ref, k3_far, half_ref, r2_ref, w3_ref, pd, rows, k3_ref, t_ref, sem):
    kernel = pltpu.make_async_copy(k3_far, k3_ref, sem)
    kernel.start()

    def shift(i, carry):
        v = p1_ref[i].astype(F32)
        pd[0, i] = pltpu.roll(v, 1, 0)
        pd[1, i] = v
        pd[2, i] = pltpu.roll(v, 23, 0)
        return carry

    lax.fori_loop(0, 10, shift, 0)
    for t in range(0, 9, 3):
        planes = []
        for dx in range(3):
            for dy in range(3):
                pieces = [pd[dy, dx : dx + 8, :, 128 * u : 128 * u + 256].reshape(192, 256) for u in range(t, t + 3)]
                planes.append(jnp.concatenate(pieces, axis=0).astype(BF16))
        r = jnp.dot(jnp.concatenate(planes, axis=1), w2_ref[...], preferred_element_type=F32)
        own = r.reshape(3, 8, 24, 256)[:, 2:6, 4:20]
        r2_ref[64 * t : 64 * t + 192, :] = own.reshape(192, 256)
        r = jnp.max(r.reshape(3, 4, 2, 24, 256), axis=2).reshape(3, 96, 256)
        for i in range(3):
            for j in range(2):
                rows[2 * i + j, 0:96] = r[i, :, j * 128 : (j + 1) * 128]
        for j in range(6):
            half_ref[2 * t + j] = paired_rows(rows, j, 48)
    kernel.wait()
    band_kernel(32, 64, 0, k3_ref, w3_ref, t_ref)


def wide_second_part(p1, w2, k3):
    return call(
        wide_second_kernel,
        [near((18, 48, 128), F32), far((576, 256), F32), near((2304, 256), BF16)],
        [(held(p1), VMEM), (w2, VMEM), (held(k3.reshape(864, 64)), ANY)],
        [((3, 10, 24, 1280), F32), ((6, 104, 128), F32), ((864, 64), BF16), ((864, 256), F32)]
        + [pltpu.SemaphoreType.DMA(())],
    )


def second_output_kernel(r2_ref, stats_ref, params_ref, f2_ref):
    normal = normaliser(jnp.sum(stats_ref[...], axis=0), VOXELS_1 / 8, params_ref, 1, 2)
    f = [settle(r2_ref[64 * t : 64 * t + 64, :], normal) for t in range(9)]
    wide = pltpu.roll(jnp.concatenate(f, axis=1), 2304 - 64, 1)[:, 0:2048]
    f2_ref[...] = wide.reshape(4, 16, 2048).astype(BF16)


def second_output(r2, stats, table):
    return call(
        second_output_kernel,
        [full((4, 16, 2048), BF16)],
        [(held(r2), VMEM), (stats, VMEM), (table, VMEM)],
    )[0]


def third_kernel(half_ref, stats_ref, params_ref, w3_ref, r3_ref, out_ref, p2, yrow):
    normal = normaliser(jnp.sum(stats_ref[...], axis=0), VOXELS_1 / 8, params_ref, 1, 1)
    bx, by, bz = position()
    pick = selector(32)
    gy = iota((12, 128), 0) - 2 + by * 8
    for j in range(9):
        pooled = halved(half_ref[2 * j], half_ref[2 * j + 1], normal, pick)
        gz = iota((12, 128), 1) // 32 + 4 * j - 1 + bz * 32
        inside = (gy >= 0) & (gy < 32) & (gz >= 0) & (gz < 128)
        for px in range(4):
            gx = px - 1 + bx * 2
            p2[px, 0:12, j * 128 : (j + 1) * 128] = jnp.where(
                inside & (gx >= 0) & (gx < 16), pooled[px * 12 : px * 12 + 12, :], 0.0
            )
    planes = []
    for dx in range(3):
        for dy in range(3):
            pieces = []
            for t in range(8):
                for x in range(2):
                    pieces.append(p2[x + dx, 1 + dy : 9 + dy, 128 * t : 128 * t + 256])
            planes.append(jnp.concatenate(pieces, axis=0).astype(BF16))
    r = jnp.dot(jnp.concatenate(planes, axis=1), w3_ref[...], preferred_element_type=F32)
    r3_ref[...] = r
    s1 = fold(jnp.sum(r, axis=0, keepdims=True), 64)
    s2 = fold(jnp.sum(r * r, axis=0, keepdims=True), 64)
    low = iota((8, 128), 1) < 64
    for t in range(8):
        m = jnp.maximum(r[t * 16 : t * 16 + 8, :], r[t * 16 + 8 : t * 16 + 16, :])
        a, b = m[:, 0:128], m[:, 128:256]
        a = jnp.maximum(a, pltpu.roll(a, 64, 1))
        b = jnp.maximum(b, pltpu.roll(b, 64, 1))
        yrow[:, t * 128 : (t + 1) * 128] = jnp.where(low, a, b)
    pooled = jnp.concatenate(
        [jnp.maximum(yrow[2 * i : 2 * i + 1, :], yrow[2 * i + 1 : 2 * i + 2, :]) for i in range(4)], axis=0
    )
    mean_here = s1 / 512.0
    spread = jnp.sqrt(jnp.maximum(s2 / 512.0 - mean_here * mean_here, 0.0))
    begin = mean_here + jnp.clip(-params_ref[5:6, :] / params_ref[4:5, :], -8.0, 8.0) * spread
    offset = jnp.maximum(begin, fold(jnp.sum(pooled, axis=0, keepdims=True), 64) / 64.0)
    at = iota((1, 128), 1)
    offset = offset.astype(BF16).astype(F32)
    apart = pooled - jnp.concatenate([offset] * 8, axis=1)
    wide = pltpu.roll(jnp.concatenate([apart, jnp.zeros((4, 128), F32)], axis=1), 64, 1)
    sums = jnp.where(at < 64, s1, s2)
    high = sums.astype(BF16).astype(F32)
    middle = (sums - high).astype(BF16).astype(F32)
    edge = jnp.concatenate([high, middle, sums - high - middle, offset], axis=0)
    ends = iota((4, 128), 1) < 64
    out = jnp.concatenate(
        [jnp.where(ends, edge, wide[:, 0:128]), wide[:, 128:1024], jnp.where(ends, wide[:, 1024:1152], edge)], axis=1
    ).astype(BF16)
    out_ref[...] = jnp.broadcast_to(out.reshape(1, 4, 1152), (DEVICES // 2, 4, 1152))


def third_part(half, stats, table, w3):
    return call(
        third_kernel,
        [near((128, 256), F32), far((DEVICES // 2, 4, 1152), BF16)],
        [(a, VMEM) for a in (half, stats, table, w3)],
        [((4, 16, 1152), F32), ((8, 1024), F32)],
    )


def fourth_kernel(r3_ref, own_ref, other_ref, params_ref, w4_ref, f3_ref, out_far, p3, pd, r4, out_ref, sems):
    edge = jnp.zeros((4, 128), F32)
    tail = jnp.zeros((4, 128), F32)
    for ref in (own_ref, other_ref):
        edge = edge + jnp.sum(ref[:, :, 0:128].astype(F32), axis=0)
        tail = tail + jnp.sum(ref[:, :, 1024:1152].astype(F32), axis=0)
    total = jnp.sum(jnp.where(iota((4, 128), 1) < 64, edge, tail)[0:3, :], axis=0, keepdims=True)
    normal = normaliser(total, VOXELS_1 / 64, params_ref, 2, 2)
    f3 = settle(r3_ref[...], normal)
    for t in range(8):
        for x in range(2):
            f3_ref[x, :, t * 256 : (t + 1) * 256] = f3[t * 16 + x * 8 : t * 16 + x * 8 + 8, :].astype(BF16)
    lane = iota((4, 128), 1)
    low = iota((16, 128), 1) < 64
    y = iota((16, 128), 0)
    one = tuple(v[:, 0:128] for v in normal)
    zero = jnp.zeros((16, 4224), BF16)
    for dy in range(3):
        pd[dy, 0] = zero
        pd[dy, 9] = zero

    first_core = lax.axis_index("gc") == 0

    def place(gx):
        for gh in range(2):
            last = [jnp.zeros((4, 128), F32)] * 2
            for gz in range(4):
                block = (gx * 2 + gh) * 4 + gz
                mine, theirs = own_ref[block].astype(F32), other_ref[block].astype(F32)
                start = gz * 1024
                for gc, v in enumerate((jnp.where(first_core, mine, theirs), jnp.where(first_core, theirs, mine))):
                    y0 = 8 * gh + 4 * gc
                    v0, v8 = v[:, 0:128], v[:, 1024:1152]
                    offset = jnp.where(lane < 64, v0, v8)[3:4, :]
                    p3[gx % 2, y0 : y0 + 4, start : start + 128] = jnp.where(lane < 64, last[gc], v0 + offset)
                    p3[gx % 2, y0 : y0 + 4, start + 128 : start + 1024] = v[:, 128:1024] + jnp.concatenate([offset] * 7, axis=1)
                    last[gc] = v8 + offset
            for gc in range(2):
                p3[gx % 2, 8 * gh + 4 * gc : 8 * gh + 4 * gc + 4, 4096:4224] = last[gc]
        for j in range(33):
            lanes = slice(j * 128, (j + 1) * 128)
            v = settle(p3[gx % 2, :, lanes], one)
            if j == 0:
                v = jnp.where(low, 0.0, v)
            if j == 32:
                v = jnp.where(low, v, 0.0)
            pd[0, gx + 1, :, lanes] = jnp.where(y > 0, pltpu.roll(v, 1, 0), 0.0).astype(BF16)
            pd[1, gx + 1, :, lanes] = v.astype(BF16)
            pd[2, gx + 1, :, lanes] = jnp.where(y < 15, pltpu.roll(v, 15, 0), 0.0).astype(BF16)

    def multiply(x0, count, t0, tiles, sums):
        planes = []
        for dx in range(3):
            for dy in range(3):
                pieces = [
                    pd[dy, x0 + dx : x0 + dx + count, :, 128 * t : 128 * t + 256].reshape(count * 16, 256)
                    for t in range(t0, t0 + tiles)
                ]
                planes.append(jnp.concatenate(pieces, axis=0))
        r = jnp.dot(jnp.concatenate(planes, axis=1), w4_ref[...], preferred_element_type=F32)
        for i in range(tiles):
            at = (t0 + i) * 128 + x0 * 16
            r4[at : at + count * 16, :] = r[i * count * 16 : (i + 1) * count * 16]
        return sums[0] + jnp.sum(r, axis=0, keepdims=True), sums[1] + jnp.sum(r * r, axis=0, keepdims=True)

    sums = (jnp.zeros((1, 256), F32), jnp.zeros((1, 256), F32))
    for gx in range(8):
        place(gx)
        if gx % 2 == 0 and gx:
            for t in (0, 16):
                sums = multiply(gx - 2, 2, t, 16, sums)
    for t in (0, 16):
        sums = multiply(6, 2, t, 16, sums)
    s1, s2 = sums
    cells = VOXELS_1 / 512
    mean = fold(s1, 128) / cells
    variance = fold(s2, 128) / cells - mean * mean
    factor = params_ref[6:7, :] * lax.rsqrt(variance + EPSILON)
    last = tuple(jnp.concatenate([v] * 2, axis=1) for v in (mean, factor, params_ref[7:8, :]))

    copies = []
    for i in range(4):
        for t in range(8 * i, 8 * i + 8):
            f = settle(r4[t * 128 : t * 128 + 128, :], last).astype(BF16)
            out_ref[:, :, 256 * t : 256 * t + 256] = f.reshape(8, 16, 256)
        lanes = pl.ds(2048 * i, 2048)
        copies.append(pltpu.make_async_copy(out_ref.at[:, :, lanes], out_far.at[:, :, lanes], sems.at[i]))
        copies[i].start()
    for c in copies:
        c.wait()


def fourth_part(r3, own, other, table, w4):
    return call(
        fourth_kernel,
        [full((2, 8, 2048), BF16), far((8, 16, 8192), BF16)],
        [(a, VMEM) for a in (r3, own, other, table, w4)],
        [((2, 16, 4224), F32), ((3, 10, 16, 4224), BF16), ((4096, 256), F32), ((8, 16, 8192), BF16)]
        + [pltpu.SemaphoreType.DMA((4,))],
        [VMEM, ANY],
    )


def across(block, axis, swaps):
    return lax.ppermute(block, axis, swaps + [(b, a) for a, b in swaps])


def after(values, event):
    return lax.optimization_barrier((values, event))


def shards(volume, k1, g1, b1, k2, g2, b2, k3, g3, b3, k4, g4, b4):
    outer = across(volume, "gz", [(1, 2)])
    inner = across(volume, "gz", [(0, 1), (2, 3)])
    w1, w1_far, block = first_band(k1, volume)
    (inner, outer, w1) = lax.optimization_barrier((inner, outer, w1))
    wide, outer = widen(block, inner, outer)
    (wide, outer, k2) = lax.optimization_barrier((wide, outer, k2))
    outer = across(outer, ("gh", "gc"), [(1, 2)])
    inner = across(inner_face(wide), "gc", [(0, 1)])
    mid, inner, outer = assemble(wide, inner, outer)
    (mid, k2) = lax.optimization_barrier((mid, k2))
    inner = across(inner, "gx", [(0, 1), (2, 3), (4, 5), (6, 7)])
    outer = across(outer, "gx", [(1, 2), (3, 4), (5, 6)])
    w2, table = early_part(k2, (g1, b1, g2, b2, g3, b3, g4, b4))
    lhs_mid, far_mid, sums = middle_part(mid, w1)
    (inner, outer, lhs_mid, w2) = lax.optimization_barrier((inner, outer, lhs_mid, w2))
    ends, sides, stats = first_part(inner, outer, lhs_mid, sums, w1)

    total1 = lax.all_to_all(stats, AXES, 0, 0, tiled=True)
    half1 = wide_first_part(sides, far_mid, ends, w1_far)
    half1, total1 = after(half1, total1)
    p1, stats = second_part(half1, total1, table, w2)

    p1, stats = after(p1, stats)
    total2 = lax.all_to_all(stats, AXES, 0, 0, tiled=True)
    half2, r2, w3 = wide_second_part(p1, w2, k3)
    (half2, w3), total2 = after((half2, w3), total2)
    r3, packed = third_part(half2, total2, table, w3)

    (k4, far_mid, r2), packed = after((k4, far_mid, r2), packed)
    own = lax.all_to_all(packed, CHIPS, 0, 0, tiled=True)
    f1 = first_output(far_mid, ends, w1_far, total1, table)
    f2 = second_output(r2, total2, table)
    w4 = band(k4, 0)
    (f1, f2, w4), own = after((f1, f2, w4), own)
    other = lax.ppermute(own, "gc", [(0, 1), (1, 0)])
    f3, f4 = fourth_part(r3, own, other, table, w4)
    return f1, f2, f3, f4


def solution(mesh):
    parts = Mesh(mesh.devices.reshape(8, 2, 2, 4), AXES)
    spread = P("gx", ("gh", "gc"), "gz")
    return jax.shard_map(
        shards,
        mesh=parts,
        in_specs=(spread,) + (P(),) * 12,
        out_specs=(spread, spread, spread, P()),
        check_vma=False,
    )
```
